32 devices in a mesh: dp: 2 (over y), seq: 4 (over z), tensor: 4 (over x, core).
Axes of the slice: x: 2, y: 2, z: 4, core: 2. Of those that a mesh axis runs over, the one named last changes fastest.
Arguments:
- residual: bfloat16 [4, 2048, 1024], P('dp', 'seq'), may hold values from -6 to 6
- block_order: int32 [4, 8], P('dp'), may hold values from 0 to 7, each once within a row
- projections: bfloat16 [3, 1024, 1024], P(None, None, 'tensor'), may hold values from -0.25 to 0.25
- offsets: float32 [3, 1024], P(None, 'tensor'), may hold values from -0.9 to 0.9
- mixing: bfloat16 [1024, 1024], P('tensor'), may hold values from -1.5 to 1.5
- baseline: float32 [1024], replicated, may hold values from -1.8 to 1.8
- expand: bfloat16 [1024, 4096], P(None, 'tensor'), may hold values from -0.1875 to 0.1875
- thresholds: float32 [4096], P('tensor'), may hold values from -3 to 3
- contract: bfloat16 [4096, 1024], P('tensor'), may hold values from -0.09375 to 0.09375
- norm_scale: float32 [2, 1024], replicated, may hold values from 0.1 to 1.9
- norm_shift: float32 [2, 1024], replicated, may hold values from -1.8 to 1.8
- cotangent: bfloat16 [4, 2048, 1024], P('dp', 'seq'), may hold values from -6 to 6
Outputs:
- layer_output: bfloat16 [4, 2048, 1024], P('dp', 'seq')
- grad_residual: bfloat16 [4, 2048, 1024], P('dp', 'seq')
- grad_projections: float32 [3, 1024, 1024], P(None, None, 'tensor')
- grad_offsets: float32 [3, 1024], P(None, 'tensor')
- grad_mixing: float32 [1024, 1024], P('tensor')
- grad_baseline: float32 [1024], replicated
- grad_expand: float32 [1024, 4096], P(None, 'tensor')
- grad_thresholds: float32 [4096], P('tensor')
- grad_contract: float32 [4096, 1024], P('tensor')
- grad_scale: float32 [2, 1024], replicated
- grad_shift: float32 [2, 1024], replicated
The draws below stay inside these ranges and needn't reach their ends.
Inputs may be any that keep to these rules, and one draw needn't show every extreme that they name: Each row of block_order holds every number of 0 to 7 once.
All inputs are finite; a program needn't handle non-finite values.
Results may differ from the reference program's by a relative error of at most 0.017.
Values may be sent and summed in bfloat16 or wider, within the bound.
No kernel may reach another device: no remote copies, remote signals or barrier semaphores. Data moves between devices by JAX's collectives and lax.ppermute only.
A program may use at most 320 MiB of HBM per device.

```python
import jax
import jax.numpy as jnp
from jax import lax

HEAD_DIM = 64
ROT = 16
FF = 4096
D = 1024
SPAN = 256
LEN = 2048
BATCH = 4
N_TENSOR = 4


def shard_levels(own_key, extent, shards, least, largest):
    factor_of = 1.0
    for position, shards_of in shards:
        draws = jax.random.uniform(jax.random.fold_in(jax.random.fold_in(own_key, 6), position), (shards_of,), jnp.float32, least / len(shards), largest / len(shards))
        factor_of = factor_of * jnp.repeat(jnp.exp(draws), extent[position] // shards_of).reshape((-1,) + (1,) * (len(extent) - 1 - position))
    return factor_of


def scatter_about(key, extent, scale, limit, shards=(), held_as=jnp.bfloat16):
    values = scale * jax.random.normal(key, extent, jnp.float32)
    if shards:
        values = values * shard_levels(key, extent, shards, -0.22, 0.18)
    return jnp.clip(values, -limit, limit).astype(held_as)


def setup_inputs(seed: int = 0) -> dict:
    arg_keys = jax.random.split(jax.random.key(seed), 13)
    return {
        "residual": scatter_about(arg_keys[0], (BATCH, LEN, D), 1.0, 6.0, ((0, 2), (1, 4))),
        "block_order": jax.vmap(lambda own: jax.random.permutation(own, LEN // SPAN))(jax.random.split(arg_keys[1], BATCH)).reshape((BATCH, LEN // SPAN)).astype(jnp.int32),
        "projections": scatter_about(arg_keys[2], (3, D, D), (D // 2) ** -0.5, 0.25, ((2, 4),)),
        "offsets": scatter_about(arg_keys[3], (3, D), 0.15, 0.9, ((1, 4),), jnp.float32),
        "mixing": scatter_about(arg_keys[4], (D, D), (D // 64) ** -0.5, 1.5, ((0, 4),)),
        "baseline": scatter_about(arg_keys[5], (D,), 0.3, 1.8, (), jnp.float32),
        "expand": scatter_about(arg_keys[6], (D, FF), D ** -0.5, 0.1875, ((1, 4),)),
        "thresholds": scatter_about(arg_keys[7], (FF,), 0.5, 3.0, ((0, 4),), jnp.float32),
        "contract": scatter_about(arg_keys[8], (FF, D), FF ** -0.5, 0.09375, ((0, 4),)),
        "norm_scale": jnp.clip(1.0 + 0.18 * jax.random.normal(arg_keys[9], (2, D), jnp.float32), 0.1, 1.9),
        "norm_shift": scatter_about(arg_keys[10], (2, D), 0.3, 1.8, (), jnp.float32),
        "cotangent": scatter_about(arg_keys[11], (BATCH, LEN, D), 1.0, 6.0, ((0, 2), (1, 4))),
    }


@jax.custom_vjp
def low(v):
    return lax.optimization_barrier(v.astype(jnp.bfloat16)).astype(jnp.float32)

@jax.custom_vjp
def low_back(v):
    return v

def low_keep(v):
    return (low(v), None)

def low_pass(kept, grad):
    return (grad,)

def back_keep(v):
    return (v, None)

def back_low(kept, grad):
    return (low(grad),)
low.defvjp(low_keep, low_pass)
low_back.defvjp(back_keep, back_low)
norm_eps = 1e-05
masked_value = -1e+30
highest = lax.Precision.HIGHEST

def normalize(values):
    centred = values - lax.optimization_barrier(jnp.mean(values, axis=-1, keepdims=True))
    inverse = lax.rsqrt(lax.optimization_barrier(jnp.mean(centred * centred, axis=-1, keepdims=True)) + norm_eps)
    return (centred * inverse, inverse)

def rotate(values, positions, rot_dims, direction):
    half_dims = rot_dims // 2
    freqs = 10000.0 ** (-jnp.arange(half_dims, dtype=jnp.float32) * 2.0 / rot_dims)
    angles = positions.astype(jnp.float32)[:, :, None] * freqs
    cosine = jnp.cos(angles)[:, :, None, :]
    sine = direction * jnp.sin(angles)[:, :, None, :]
    first = values[..., :half_dims]
    second = values[..., half_dims:rot_dims]
    return jnp.concatenate([first * cosine - second * sine, second * cosine + first * sine, values[..., rot_dims:]], axis=-1)

def group_branch(attn_low, feed_low, positions, weights):
    projection, offset, mixing_part, expand_part, threshold_part, contract_part = weights
    head_count = projection.shape[2] // HEAD_DIM
    attn_in = low_back(attn_low)
    linear = jnp.einsum('rd,ide->ire', attn_in, projection, precision=highest) + offset[:, None, :]
    linear = low_back(linear)
    split_shape = (1, LEN, head_count, HEAD_DIM)
    queries = low(rotate(linear[0].reshape(split_shape), positions[None], ROT, 1.0))[0]
    keys = low(rotate(linear[1].reshape(split_shape), positions[None], ROT, 1.0))[0]
    values = low(linear[2]).reshape(LEN, head_count, HEAD_DIM)
    scores = low_back(jnp.einsum('qhe,khe->hqk', queries, keys, precision=highest)) * HEAD_DIM ** (-0.5)
    causal = positions[None, None, :] <= positions[None, :, None]
    probs = low(jax.nn.softmax(jnp.where(causal, scores, masked_value), axis=-1))
    attended = jnp.einsum('hqk,khe->qhe', probs, values, precision=highest).reshape(LEN, head_count * HEAD_DIM)
    attended = low(low_back(attended))
    feed_in = low_back(feed_low)
    hidden = low_back(jnp.dot(feed_in, expand_part, precision=highest) + threshold_part)
    activated = low(jax.nn.gelu(hidden, approximate=False))
    return low(jnp.dot(attended, mixing_part, precision=highest) + jnp.dot(activated, contract_part, precision=highest))

def one_sequence(params, residual_row, positions):
    projections, offsets, mixing, baseline, expand, thresholds, contract, norm_scale, norm_shift = params
    normed, inverse = normalize(residual_row)
    attn_low = low(normed * norm_scale[0] + norm_shift[0])
    feed_low = low(normed * norm_scale[1] + norm_shift[1])
    groups = N_TENSOR
    local_width = D // groups
    local_hidden = FF // groups
    grouped = (projections.reshape(3, D, groups, local_width).transpose(2, 0, 1, 3), offsets.reshape(3, groups, local_width).transpose(1, 0, 2), mixing.reshape(groups, local_width, D), expand.reshape(D, groups, local_hidden).transpose(1, 0, 2), thresholds.reshape(groups, local_hidden), contract.reshape(groups, local_hidden, D))

    def branch(weights):
        return group_branch(attn_low, feed_low, positions, weights)
    parts = lax.map(jax.checkpoint(branch), grouped)
    return residual_row + lax.optimization_barrier(jnp.sum(parts, axis=0)) + baseline

def forward(params, inputs, positions):

    def per_sequence(pair):
        return one_sequence(params, pair[0], pair[1])
    return lax.map(jax.checkpoint(per_sequence), (inputs, positions))

def reference(residual, block_order, projections, offsets, mixing, baseline, expand, thresholds, contract, norm_scale, norm_shift, cotangent):
    positions = (block_order[:, :, None] * SPAN + jnp.arange(SPAN, dtype=jnp.int32)[None, None, :]).reshape(block_order.shape[0], LEN).astype(jnp.int32)
    params = (projections.astype(jnp.float32), offsets.astype(jnp.float32), mixing.astype(jnp.float32), baseline.astype(jnp.float32), expand.astype(jnp.float32), thresholds.astype(jnp.float32), contract.astype(jnp.float32), norm_scale.astype(jnp.float32), norm_shift.astype(jnp.float32))
    inputs = residual.astype(jnp.float32)

    def run(params_in, inputs_in):
        return forward(params_in, inputs_in, positions)
    output, pullback = jax.vjp(run, params, inputs)
    grads, grad_inputs = pullback(cotangent.astype(jnp.float32))
    grad_projections, grad_offsets, grad_mixing, grad_baseline, grad_expand, grad_thresholds, grad_contract, grad_scale, grad_shift = grads
    return (output.astype(jnp.bfloat16), grad_inputs.astype(jnp.bfloat16), grad_projections, grad_offsets, grad_mixing, grad_baseline, grad_expand, grad_thresholds, grad_contract, grad_scale, grad_shift)
```

```python
import functools

import jax
import jax.numpy as jnp
import numpy as np
from jax import lax
from jax.experimental import pallas as pl
from jax.experimental.pallas import tpu as pltpu
from jax.sharding import PartitionSpec as P

HEAD_DIM = 64
ROT = 16
LANES = 128

norm_eps = 1e-05
masked_value = -1e30
low = jnp.bfloat16
wide = jnp.float32


def dot_nn(a, b):
    return lax.dot_general(a, b, (((1,), (0,)), ((), ())), preferred_element_type=wide)


def dot_nt(a, b):
    return lax.dot_general(a, b, (((1,), (1,)), ((), ())), preferred_element_type=wide)


def rotary_tables(length):
    half = ROT // 2
    freqs = np.float32(10000.0) ** (-np.arange(half, dtype=np.float32) * 2.0 / ROT)
    angles = np.arange(length, dtype=np.float32)[:, None] * freqs.astype(np.float32)
    cosine = np.ones((length, HEAD_DIM), np.float32)
    sine = np.zeros((length, HEAD_DIM), np.float32)
    cosine[:, :half] = np.cos(angles)
    cosine[:, half:ROT] = np.cos(angles)
    sine[:, :half] = -np.sin(angles)
    sine[:, half:ROT] = np.sin(angles)
    return np.tile(cosine, (1, LANES // HEAD_DIM)), np.tile(sine, (1, LANES // HEAD_DIM))


def rotate_lanes(x, cosine, sine):
    width = x.shape[1]
    if width < LANES:
        x = jnp.concatenate([x, x], axis=1)
    lane = lax.broadcasted_iota(jnp.int32, x.shape, 1) % HEAD_DIM
    partner = jnp.where(
        lane < ROT // 2, pltpu.roll(x, LANES - ROT // 2, 1), pltpu.roll(x, ROT // 2, 1)
    )
    return (x * cosine + partner * sine)[:, :width]


def project_kernel(
    places, res, cot, proj, offs, mix, scale, shift, cosine, sine, out, attn_out, feed_out
):
    x = res[0].astype(wide)
    centred = x - jnp.mean(x, axis=1, keepdims=True)
    inverse = lax.rsqrt(jnp.mean(centred * centred, axis=1, keepdims=True) + norm_eps)
    normed = centred * inverse
    attn_in = (normed * scale[0:1] + shift[0:1]).astype(low)
    attn_out[0] = attn_in
    feed_out[0] = (normed * scale[1:2] + shift[1:2]).astype(low)
    parts, width = out.shape[0], out.shape[4]
    for i in range(3):
        linear = dot_nn(attn_in, proj[i]) + offs[i : i + 1]
        if i < 2:
            linear = jnp.concatenate(
                [
                    rotate_lanes(linear[:, c : c + LANES], cosine[...], sine[...])
                    for c in range(0, linear.shape[1], LANES)
                ],
                axis=1,
            )
        linear = linear.astype(low)
        for w in range(parts):
            out[w, i, 0] = linear[:, w * width : (w + 1) * width]
    grad = dot_nt(cot[0], mix[...]).astype(low)
    for w in range(parts):
        out[w, 3, 0] = grad[:, w * width : (w + 1) * width]


def project(residual, cotangent, places, projections, offsets, mixing, scale, shift, tables, dims):
    blocks, span, model = residual.shape
    n, per_device, width = dims
    local = projections.shape[2]
    parts = local // width
    whole = lambda *shape: pl.BlockSpec(shape, lambda t, p: (0,) * len(shape))
    token = pl.BlockSpec((1, span, model), lambda t, p: (t, 0, 0))
    table = pl.BlockSpec((span, LANES), lambda t, p: (p[t], 0))
    return pl.pallas_call(
        project_kernel,
        grid_spec=pltpu.PrefetchScalarGridSpec(
            num_scalar_prefetch=1,
            grid=(blocks,),
            in_specs=[
                token,
                token,
                whole(3, model, local),
                whole(3, local),
                whole(local, model),
                whole(2, model),
                whole(2, model),
                table,
                table,
            ],
            out_specs=[
                pl.BlockSpec(
                    (parts, 4, 1, span, width),
                    lambda t, p: (t // per_device, 0, t % per_device, 0, 0),
                ),
                token,
                token,
            ],
        ),
        out_shape=[
            jax.ShapeDtypeStruct((n, 4, per_device, span, width), low),
            jax.ShapeDtypeStruct((blocks, span, model), low),
            jax.ShapeDtypeStruct((blocks, span, model), low),
        ],
        compiler_params=pltpu.CompilerParams(vmem_limit_bytes=40 * 2**20),
    )(places, residual, cotangent, projections, offsets, mixing, scale, shift, *tables)


def attention_kernel(n, per_device, slots, *refs):
    received, refs = refs[:n], refs[n:]
    cosine, sine = refs[0], refs[1]
    outs_o, refs = refs[2 : 2 + n], refs[2 + n :]
    outs_d, refs = refs[:n], refs[n:]
    xs, ys_o, ys_d, k_turned, v_turned, strip, dk_sum, dv_sum, sems = refs
    blocks = n * per_device
    span, width = xs.shape[3], xs.shape[4]
    heads = width // HEAD_DIM
    scale = HEAD_DIM ** (-0.5)
    to_log2 = scale * float(np.log2(np.e))

    copies = [pltpu.make_async_copy(received[k], xs.at[k], sems.at[k]) for k in range(n)]
    for copy in copies:
        copy.start()
    dk_sum[...] = jnp.zeros_like(dk_sum)
    dv_sum[...] = jnp.zeros_like(dv_sum)
    for copy in copies:
        copy.wait()

    def place(j):
        slot = slots[j]
        return slot // per_device, slot % per_device

    def turn(j, _):
        a, b = place(j)
        k_turned[j] = xs[a, 1, b].astype(wide).T.astype(low)
        v_turned[j] = xs[a, 2, b].astype(wide).T.astype(low)
        return 0

    lax.fori_loop(0, blocks, turn, 0)

    lane_head = lax.broadcasted_iota(jnp.int32, (span, width), 1) // HEAD_DIM

    def stacked(x):
        if heads == 1:
            return x
        return jnp.concatenate(
            [jnp.where(lane_head == h, x, jnp.zeros_like(x)) for h in range(heads)], axis=0
        )

    def head_rows(h):
        return slice(h * HEAD_DIM, (h + 1) * HEAD_DIM)

    def head_cols(h):
        return slice(h * span, (h + 1) * span)

    shape = (span, heads * span)
    allowed = lax.broadcasted_iota(jnp.int32, shape, 0) <= (
        lax.broadcasted_iota(jnp.int32, shape, 1) % span
    )

    def query_block(i, _):
        a, b = place(i)
        q, g = xs[a, 0, b], xs[a, 3, b]
        q_all, g_all = stacked(q), stacked(g)
        g_turned = g.astype(wide).T

        own = jnp.where(allowed, dot_nt(xs[a, 1, b], q_all), masked_value)
        strip[i] = own
        top = jnp.max(own, axis=0, keepdims=True)

        def scores(j, top):
            c, d = place(j)
            s = dot_nt(xs[c, 1, d], q_all)
            strip[j] = s
            return jnp.maximum(top, jnp.max(s, axis=0, keepdims=True))

        top = lax.fori_loop(0, i, scores, top)

        def weigh(j, carry):
            total, outs = carry
            p = jnp.exp2((strip[j] - top) * to_log2)
            strip[j] = p
            p_low = p.astype(low)
            return total + jnp.sum(p, axis=0, keepdims=True), tuple(
                outs[h] + dot_nn(v_turned[j, head_rows(h)], p_low[:, head_cols(h)])
                for h in range(heads)
            )

        zeros = tuple(jnp.zeros((HEAD_DIM, span), wide) for _ in range(heads))
        total, outs = lax.fori_loop(
            0, i + 1, weigh, (jnp.zeros((1, heads * span), wide), zeros)
        )
        recip = 1.0 / total
        outs = [outs[h] * recip[:, head_cols(h)] for h in range(heads)]
        row_dots = jnp.concatenate(
            [
                jnp.sum(outs[h] * g_turned[head_rows(h)], axis=0, keepdims=True)
                for h in range(heads)
            ],
            axis=1,
        )
        ys_o[a, b] = jnp.concatenate(outs, axis=0).T.astype(low)
        slope_scale = scale * recip
        slope_shift = slope_scale * row_dots

        def back(j, dq):
            c, d = place(j)
            p = strip[j]
            dots = dot_nt(xs[c, 2, d], g_all)
            slopes = (p * (dots * slope_scale - slope_shift)).astype(low)
            dv_sum[j] += dot_nn((p * recip).astype(low), g_all)
            dk_sum[j] += dot_nn(slopes, q_all)
            return tuple(
                dq[h] + dot_nn(k_turned[j, head_rows(h)], slopes[:, head_cols(h)])
                for h in range(heads)
            )

        dq = lax.fori_loop(0, i + 1, back, zeros)
        dq = jnp.concatenate(dq, axis=0).T
        rows = pl.ds(pl.multiple_of(i * span, span), span)
        ys_d[a, 0, b] = rotate_lanes(dq, cosine[rows], -sine[rows]).astype(low)
        return 0

    lax.fori_loop(0, blocks, query_block, 0)

    def finish(j, _):
        a, b = place(j)
        rows = pl.ds(pl.multiple_of(j * span, span), span)
        ys_d[a, 1, b] = rotate_lanes(dk_sum[j], cosine[rows], -sine[rows]).astype(low)
        ys_d[a, 2, b] = dv_sum[j].astype(low)
        return 0

    lax.fori_loop(0, blocks, finish, 0)
    copies = [pltpu.make_async_copy(ys_o.at[k], outs_o[k], sems.at[k]) for k in range(n)]
    copies += [pltpu.make_async_copy(ys_d.at[k], outs_d[k], sems.at[n + k]) for k in range(n)]
    for copy in copies:
        copy.start()
    for copy in copies:
        copy.wait()


def attention(received, slots, tables, per_device):
    n = len(received)
    _, _, span, width = received[0].shape
    blocks = n * per_device
    heads = width // HEAD_DIM
    anywhere = pl.BlockSpec(memory_space=pl.ANY)
    vmem = pl.BlockSpec(memory_space=pltpu.VMEM)
    pairs = blocks * (blocks + 1) // 2 * heads * span * span
    results = pl.pallas_call(
        functools.partial(attention_kernel, n, per_device),
        in_specs=[pl.BlockSpec(memory_space=pltpu.SMEM)] + [anywhere] * n + [vmem] * 2,
        out_specs=[anywhere] * (2 * n),
        out_shape=[jax.ShapeDtypeStruct((per_device, span, width), low)] * n
        + [jax.ShapeDtypeStruct((3, per_device, span, width), low)] * n,
        scratch_shapes=[
            pltpu.VMEM((n, 4, per_device, span, width), low),
            pltpu.VMEM((n, per_device, span, width), low),
            pltpu.VMEM((n, 3, per_device, span, width), low),
            pltpu.VMEM((blocks, width, span), low),
            pltpu.VMEM((blocks, width, span), low),
            pltpu.VMEM((blocks, span, heads * span), wide),
            pltpu.VMEM((blocks, span, width), wide),
            pltpu.VMEM((blocks, span, width), wide),
            pltpu.SemaphoreType.DMA((2 * n,)),
        ],
        compiler_params=pltpu.CompilerParams(vmem_limit_bytes=40 * 2**20),
        cost_estimate=pl.CostEstimate(
            flops=12 * pairs * 256, bytes_accessed=8 * 2**20, transcendentals=pairs
        ),
    )(slots, *received, *tables)
    return results[:n], results[n:]


def steps_over(*axes):
    steps = []
    for axis in axes:
        size = lax.axis_size(axis)
        bit = 1
        while bit < size:
            steps.append((axis, [(s, s ^ bit) for s in range(size)], bit))
            bit *= 2
    return steps


def side_of(axis, bit):
    return (lax.axis_index(axis) // bit) % 2


def reduce_rows(x, steps):
    for axis, perm, bit in steps:
        half = x.shape[0] // 2
        side = side_of(axis, bit)
        sent = lax.dynamic_slice_in_dim(x, (1 - side) * half, half, 0).astype(low)
        kept = lax.dynamic_slice_in_dim(x, side * half, half, 0)
        got = lax.ppermute(sent, axis, perm)
        x = kept.astype(wide) + got.astype(wide)
    return x


def spread_rows(x, steps):
    for axis, perm, bit in reversed(steps):
        got = lax.ppermute(x, axis, perm)
        side = side_of(axis, bit)
        x = jnp.where(
            side == 0, jnp.concatenate([x, got], axis=0), jnp.concatenate([got, x], axis=0)
        )
    return x


def own_rows(x, steps):
    for axis, _, bit in steps:
        half = x.shape[0] // 2
        x = lax.dynamic_slice_in_dim(x, side_of(axis, bit) * half, half, 0)
    return x


def sum_small(x, steps):
    for axis, perm, _ in steps:
        x = x + lax.ppermute(x, axis, perm)
    return x


def gelu_exact(values):
    return jax.nn.gelu(values, approximate=False)


def on_device(
    residual,
    block_order,
    projections,
    offsets,
    mixing,
    baseline,
    expand,
    thresholds,
    contract,
    norm_scale,
    norm_shift,
    cotangent,
):
    seq_count, local_rows, model = residual.shape
    local = mixing.shape[0]
    n = lax.axis_size("seq")
    me = lax.axis_index("seq")
    blocks = block_order.shape[1]
    length = local_rows * n
    span = length // blocks
    per_device = blocks // n
    width = seq_count * local // n
    parts = local // width
    tokens = seq_count * local_rows
    tables = [jnp.asarray(t) for t in rotary_tables(length)]

    own_blocks = lax.dynamic_slice_in_dim(block_order, me * per_device, per_device, 1).reshape(-1)
    as_blocks = (seq_count * per_device, span, model)
    sends, attn_in, feed_in = project(
        residual.reshape(as_blocks),
        cotangent.reshape(as_blocks),
        own_blocks,
        projections,
        offsets,
        mixing,
        norm_scale,
        norm_shift,
        tables,
        (n, per_device, width),
    )
    received = [lax.dynamic_index_in_dim(sends, me, 0, keepdims=False)]
    for k in range(1, n):
        part = lax.dynamic_index_in_dim(sends, (me + k) % n, 0, keepdims=False)
        received.append(lax.ppermute(part, "seq", [(s, (s + k) % n) for s in range(n)]))

    own_order = lax.dynamic_index_in_dim(block_order, me // parts, 0, keepdims=False)
    stored = jnp.arange(blocks, dtype=jnp.int32)
    slot_of = ((me - stored // per_device) % n) * per_device + stored % per_device
    slots = jnp.sum(
        jnp.where(own_order[None, :] == stored[:, None], slot_of[None, :], 0), axis=1
    ).astype(jnp.int32)

    attn_in = attn_in.reshape(tokens, model)
    feed_in = feed_in.reshape(tokens, model)
    upstream_low = cotangent.reshape(tokens, model)
    hidden = dot_nn(feed_in, expand) + thresholds
    activated = gelu_exact(hidden).astype(low)
    grad_activated = dot_nt(upstream_low, contract)
    grad_hidden = jax.vjp(gelu_exact, hidden)[1](grad_activated)[0].astype(low)
    feed_out = dot_nn(activated, contract)
    grad_contract = lax.dot_general(
        activated, upstream_low, (((0,), (0,)), ((), ())), preferred_element_type=wide
    )
    grad_expand = lax.dot_general(
        feed_in, grad_hidden, (((0,), (0,)), ((), ())), preferred_element_type=wide
    )
    feed_part = dot_nt(grad_hidden, expand)
    grad_thresholds = jnp.sum(grad_hidden.astype(wide), axis=0)
    grad_baseline = jnp.sum(upstream_low.astype(wide), axis=0)

    batch_steps = steps_over("dp", "seq")
    tensor_steps = steps_over("tensor")

    def total_rows(x):
        return spread_rows(reduce_rows(x, batch_steps).astype(low), batch_steps).astype(wide)

    grad_contract = total_rows(grad_contract)
    grad_expand = total_rows(grad_expand)

    outs_o, outs_d = attention(received, slots, tables, per_device)

    def returned(pieces, lead):
        full = jnp.zeros((n,) + pieces[0].shape, low)
        for k in range(n):
            piece = pieces[k]
            if k:
                piece = lax.ppermute(piece, "seq", [(s, (s - k) % n) for s in range(n)])
            full = lax.dynamic_update_index_in_dim(full, piece, (me + k) % n, 0)
        full = full.reshape((seq_count, parts, lead, per_device, span, width))
        return full.transpose(2, 0, 3, 4, 1, 5).reshape(lead, tokens, local)

    attended = returned(outs_o, 1)[0]
    grad_linear = returned(outs_d, 3)

    partial_out = dot_nn(attended, mixing) + feed_out
    grad_mixing = lax.dot_general(
        attended, upstream_low, (((0,), (0,)), ((), ())), preferred_element_type=wide
    )
    flat_residual = residual.reshape(tokens, model)
    branch_total = reduce_rows(partial_out, tensor_steps)
    shard_in = own_rows(flat_residual, tensor_steps).astype(wide)
    layer_output = spread_rows(
        (shard_in + branch_total + baseline).astype(low), tensor_steps
    ).reshape(residual.shape)

    grad_projections = jnp.stack(
        [
            lax.dot_general(
                attn_in, grad_linear[i], (((0,), (0,)), ((), ())), preferred_element_type=wide
            )
            for i in range(3)
        ]
    )
    grad_offsets = jnp.sum(grad_linear.astype(wide), axis=1)
    attn_part = sum(dot_nt(grad_linear[i], projections[i]) for i in range(3))

    inputs = flat_residual.astype(wide)
    centred = inputs - jnp.mean(inputs, axis=-1, keepdims=True)
    inverse = lax.rsqrt(jnp.mean(centred * centred, axis=-1, keepdims=True) + norm_eps)
    normed = centred * inverse
    upstream_part = attn_part * norm_scale[0] + feed_part * norm_scale[1]
    small_all = jnp.stack(
        [
            jnp.sum(attn_part * normed, axis=0),
            jnp.sum(feed_part * normed, axis=0),
            jnp.sum(attn_part, axis=0),
            jnp.sum(feed_part, axis=0),
        ]
    )
    combined = reduce_rows(upstream_part, tensor_steps)
    normed_own = own_rows(normed, tensor_steps)
    inverse_own = own_rows(inverse, tensor_steps)
    grad_own = own_rows(upstream_low, tensor_steps).astype(wide) + inverse_own * (
        combined
        - jnp.mean(combined, axis=-1, keepdims=True)
        - normed_own * jnp.mean(combined * normed_own, axis=-1, keepdims=True)
    )
    grad_residual = spread_rows(grad_own.astype(low), tensor_steps).reshape(residual.shape)

    grad_projections = total_rows(grad_projections.reshape(3 * model, local)).reshape(
        3, model, local
    )
    grad_mixing = total_rows(grad_mixing)
    small_all = sum_small(small_all, tensor_steps)
    small = jnp.concatenate(
        [
            small_all.reshape(-1),
            grad_offsets.reshape(-1),
            grad_thresholds,
            grad_baseline,
        ]
    )
    small = sum_small(small, batch_steps)
    sizes = [2 * model, 2 * model, 3 * local, thresholds.shape[0], model]
    grad_scale, grad_shift, grad_offsets, grad_thresholds, grad_baseline = jnp.split(
        small, np.cumsum(sizes)[:-1]
    )
    return (
        layer_output,
        grad_residual,
        grad_projections,
        grad_offsets.reshape(3, local),
        grad_mixing,
        grad_baseline,
        grad_expand,
        grad_thresholds,
        grad_contract,
        grad_scale.reshape(2, model),
        grad_shift.reshape(2, model),
    )


def solution(mesh):
    in_specs = (
        P("dp", "seq", None),
        P("dp", None),
        P(None, None, "tensor"),
        P(None, "tensor"),
        P("tensor", None),
        P(),
        P(None, "tensor"),
        P("tensor"),
        P("tensor", None),
        P(),
        P(),
        P("dp", "seq", None),
    )
    out_specs = (
        P("dp", "seq", None),
        P("dp", "seq", None),
        P(None, None, "tensor"),
        P(None, "tensor"),
        P("tensor", None),
        P(),
        P(None, "tensor"),
        P("tensor"),
        P("tensor", None),
        P(),
        P(),
    )
    return jax.shard_map(
        on_device, mesh=mesh, in_specs=in_specs, out_specs=out_specs, check_vma=False
    )
```

```python
import functools

import jax
import jax.numpy as jnp
import numpy as np
from jax import lax
from jax.experimental import pallas as pl
from jax.experimental.pallas import tpu as pltpu
from jax.sharding import PartitionSpec as P

HEAD_DIM = 64
ROT = 16
LANES = 128

norm_eps = 1e-05
masked_value = -1e30
low = jnp.bfloat16
wide = jnp.float32


def dot_nn(a, b):
    return lax.dot_general(a, b, (((1,), (0,)), ((), ())), preferred_element_type=wide)


def dot_nt(a, b):
    return lax.dot_general(a, b, (((1,), (1,)), ((), ())), preferred_element_type=wide)


def rotary_tables(length):
    half = ROT // 2
    freqs = np.float32(10000.0) ** (-np.arange(half, dtype=np.float32) * 2.0 / ROT)
    angles = np.arange(length, dtype=np.float32)[:, None] * freqs.astype(np.float32)
    cosine = np.ones((length, HEAD_DIM), np.float32)
    sine = np.zeros((length, HEAD_DIM), np.float32)
    cosine[:, :half] = np.cos(angles)
    cosine[:, half:ROT] = np.cos(angles)
    sine[:, :half] = -np.sin(angles)
    sine[:, half:ROT] = np.sin(angles)
    return np.tile(cosine, (1, LANES // HEAD_DIM)), np.tile(sine, (1, LANES // HEAD_DIM))


def rotate_lanes(x, cosine, sine):
    width = x.shape[1]
    if width < LANES:
        x = jnp.concatenate([x, x], axis=1)
    lane = lax.broadcasted_iota(jnp.int32, x.shape, 1) % HEAD_DIM
    partner = jnp.where(
        lane < ROT // 2, pltpu.roll(x, LANES - ROT // 2, 1), pltpu.roll(x, ROT // 2, 1)
    )
    return (x * cosine + partner * sine)[:, :width]


def half_lanes(shape):
    return lax.broadcasted_iota(jnp.int32, shape, 1) < HEAD_DIM


def swap_halves(x):
    return pltpu.roll(x, HEAD_DIM, 1)


def pack_heads(first, second):
    packed = []
    for c in range(0, first.shape[1], LANES):
        x, y = first[:, c : c + LANES], second[:, c : c + LANES]
        lower = half_lanes(x.shape)
        packed.append(jnp.where(lower, x, swap_halves(y)))
        packed.append(jnp.where(lower, swap_halves(x), y))
    return packed


def unpack_heads(packed):
    first, second = [], []
    for h in range(0, len(packed), 2):
        x, y = packed[h], packed[h + 1]
        lower = half_lanes(x.shape)
        first.append(jnp.where(lower, x, swap_halves(y)))
        second.append(jnp.where(lower, swap_halves(x), y))
    return jnp.concatenate(first, axis=1), jnp.concatenate(second, axis=1)


def normalize_block(x):
    centred = x - jnp.mean(x, axis=1, keepdims=True)
    inverse = lax.rsqrt(jnp.mean(centred * centred, axis=1, keepdims=True) + norm_eps)
    return centred * inverse


def project_kernel(
    places, res, cot, proj, offs, mix, scale, shift, cosine, sine, out, attn_out, feed_out
):
    normed = normalize_block(res[0].astype(wide))
    attn_in = (normed * scale[0:1] + shift[0:1]).astype(low)
    attn_out[0] = attn_in
    feed_out[0] = (normed * scale[1:2] + shift[1:2]).astype(low)
    rows = []
    for i in range(3):
        linear = dot_nn(attn_in, proj[i]) + offs[i : i + 1]
        if i < 2:
            linear = jnp.concatenate(
                [
                    rotate_lanes(linear[:, c : c + LANES], cosine[...], sine[...])
                    for c in range(0, linear.shape[1], LANES)
                ],
                axis=1,
            )
        rows.append(linear)
    rows.append(dot_nt(cot[0], mix[...]))
    for kind in range(2):
        for h, x in enumerate(pack_heads(rows[2 * kind], rows[2 * kind + 1])):
            out[h, kind, 0] = x.astype(low)


def project(residual, cotangent, places, projections, offsets, mixing, scale, shift, tables, dims):
    blocks, span, model = residual.shape
    seq_count, per_device, heads = dims
    local = projections.shape[2]
    whole = lambda *shape: pl.BlockSpec(shape, lambda t, p: (0,) * len(shape))
    token = pl.BlockSpec((1, span, model), lambda t, p: (t, 0, 0))
    table = pl.BlockSpec((span, LANES), lambda t, p: (p[t], 0))
    return pl.pallas_call(
        project_kernel,
        grid_spec=pltpu.PrefetchScalarGridSpec(
            num_scalar_prefetch=1,
            grid=(blocks,),
            in_specs=[
                token,
                token,
                whole(3, model, local),
                whole(3, local),
                whole(local, model),
                whole(2, model),
                whole(2, model),
                table,
                table,
            ],
            out_specs=[
                pl.BlockSpec(
                    (heads, 2, 1, span, LANES),
                    lambda t, p: (t // per_device, 0, t % per_device, 0, 0),
                ),
                token,
                token,
            ],
        ),
        out_shape=[
            jax.ShapeDtypeStruct((seq_count * heads, 2, per_device, span, LANES), low),
            jax.ShapeDtypeStruct((blocks, span, model), low),
            jax.ShapeDtypeStruct((blocks, span, model), low),
        ],
        compiler_params=pltpu.CompilerParams(vmem_limit_bytes=58 * 2**20),
        cost_estimate=pl.CostEstimate(
            flops=8 * blocks * span * model * local, bytes_accessed=12 * 2**20, transcendentals=0
        ),
    )(places, residual, cotangent, projections, offsets, mixing, scale, shift, *tables)


def feed_kernel(feed, cot, expand, thresholds, contract, act, grad, out, part, sums):
    hidden = dot_nn(feed[...], expand[...]) + thresholds[...]
    normal = 0.5 + 0.5 * lax.erf(hidden * float(np.sqrt(0.5)))
    density = jnp.exp(-0.5 * hidden * hidden) * float(1.0 / np.sqrt(2.0 * np.pi))
    activated = (hidden * normal).astype(low)
    act[...] = activated
    slope = normal + hidden * density
    grad_hidden = (dot_nt(cot[...], contract[...]) * slope).astype(low)
    grad[...] = grad_hidden
    out[...] = dot_nn(activated, contract[...])
    part[...] = dot_nt(grad_hidden, expand[...])

    @pl.when(pl.program_id(0) == 0)
    def _():
        sums[...] = jnp.zeros_like(sums)

    sums[0:1] += jnp.sum(grad_hidden.astype(wide), axis=0, keepdims=True)
    sums[1:2] += jnp.sum(cot[...].astype(wide), axis=0, keepdims=True)


def feed_forward(feed_in, upstream, expand, thresholds, contract, span):
    tokens, model = feed_in.shape
    units = expand.shape[1]
    whole = lambda *shape: pl.BlockSpec(shape, lambda t: (0,) * len(shape))
    rows = lambda columns: pl.BlockSpec((span, columns), lambda t: (t, 0))
    return pl.pallas_call(
        feed_kernel,
        grid=(tokens // span,),
        in_specs=[
            rows(model),
            rows(model),
            whole(model, units),
            whole(1, units),
            whole(units, model),
        ],
        out_specs=[rows(units), rows(units), rows(model), rows(model), whole(8, units)],
        out_shape=[
            jax.ShapeDtypeStruct((tokens, units), low),
            jax.ShapeDtypeStruct((tokens, units), low),
            jax.ShapeDtypeStruct((tokens, model), wide),
            jax.ShapeDtypeStruct((tokens, model), wide),
            jax.ShapeDtypeStruct((8, units), wide),
        ],
        compiler_params=pltpu.CompilerParams(vmem_limit_bytes=58 * 2**20),
        cost_estimate=pl.CostEstimate(
            flops=8 * tokens * model * units,
            bytes_accessed=20 * 2**20,
            transcendentals=2 * tokens * units,
        ),
    )(feed_in, upstream, expand, thresholds.reshape(1, units), contract)


def attention_kernel(n, per_device, slots, *refs):
    received, refs = refs[:n], refs[n:]
    cosine, sine = refs[0], refs[1]
    outs, refs = refs[2 : 2 + n], refs[2 + n :]
    xs, ys, k_lo, q_lo, v_hi, g_hi, k_turned, v_turned, strip, sums, sems = refs
    blocks = n * per_device
    span = xs.shape[3]
    tiles, big = strip.shape[0], strip.shape[1]
    ratio = big // span
    scale = HEAD_DIM ** (-0.5)
    to_log2 = scale * float(np.log2(np.e))

    copies = [pltpu.make_async_copy(received[k], xs.at[k], sems.at[k]) for k in range(n)]
    for copy in copies:
        copy.start()
    sums[...] = jnp.zeros_like(sums)
    for copy in copies:
        copy.wait()

    def place(j):
        slot = slots[j]
        return slot // per_device, slot % per_device

    def rows_of(u, size):
        return pl.ds(pl.multiple_of(u * size, size), size)

    lower = half_lanes((span, LANES))

    def order(j, _):
        a, b = place(j)
        rows = rows_of(j, span)
        x, y = xs[a, 0, b].astype(wide), xs[a, 1, b].astype(wide)
        k_lo[rows] = swap_halves(x).astype(low)
        q_lo[rows] = jnp.where(lower, x, 0.0).astype(low)
        v_hi[rows] = swap_halves(y).astype(low)
        g_hi[rows] = jnp.where(lower, 0.0, y).astype(low)
        return 0

    lax.fori_loop(0, blocks, order, 0)

    def turn(u, _):
        rows = rows_of(u, big)
        k_turned[u] = k_lo[rows].astype(wide).T[:HEAD_DIM].astype(low)
        v_turned[u] = v_hi[rows].astype(wide).T[HEAD_DIM:].astype(low)
        return 0

    lax.fori_loop(0, tiles, turn, 0)
    allowed = lax.broadcasted_iota(jnp.int32, (big, big), 0) <= lax.broadcasted_iota(
        jnp.int32, (big, big), 1
    )
    lower_big = half_lanes((big, LANES))

    def query_tile(u, _):
        own = rows_of(u, big)
        q, g = q_lo[own], g_hi[own]
        g_turned = g.astype(wide).T[HEAD_DIM:]

        s = jnp.where(allowed, dot_nt(k_lo[own], q), masked_value)
        strip[u] = s
        top = jnp.max(s, axis=0, keepdims=True)

        def scores(j, top):
            s = dot_nt(k_lo[rows_of(j, big)], q)
            strip[j] = s
            return jnp.maximum(top, jnp.max(s, axis=0, keepdims=True))

        top = lax.fori_loop(0, u, scores, top)

        def weigh(j, carry):
            total, out = carry
            p = jnp.exp2((strip[j] - top) * to_log2)
            strip[j] = p
            return total + jnp.sum(p, axis=0, keepdims=True), out + dot_nn(
                v_turned[j], p.astype(low)
            )

        zeros = jnp.zeros((HEAD_DIM, big), wide)
        total, out = lax.fori_loop(0, u + 1, weigh, (jnp.zeros((1, big), wide), zeros))
        recip = 1.0 / total
        out = out * recip
        slope_scale = scale * recip
        slope_shift = slope_scale * jnp.sum(out * g_turned, axis=0, keepdims=True)

        def back(j, dq):
            p = strip[j]
            dots = dot_nt(v_hi[rows_of(j, big)], g)
            slopes = (p * (dots * slope_scale - slope_shift)).astype(low)
            sums[j] += dot_nn(slopes, q) + dot_nn((p * recip).astype(low), g)
            return dq + dot_nn(k_turned[j], slopes)

        dq = lax.fori_loop(0, u + 1, back, zeros)
        packed = jnp.concatenate([out, dq], axis=0).T
        packed = jnp.where(lower_big, packed, rotate_lanes(packed, cosine[own], -sine[own]))
        packed = packed.astype(low)
        for t in range(ratio):
            a, b = place(u * ratio + t)
            ys[a, 0, b] = packed[t * span : (t + 1) * span]
        return 0

    lax.fori_loop(0, tiles, query_tile, 0)

    def finish(u, _):
        own = rows_of(u, big)
        x = sums[u]
        packed = jnp.where(lower_big, rotate_lanes(x, cosine[own], -sine[own]), x).astype(low)
        for t in range(ratio):
            a, b = place(u * ratio + t)
            ys[a, 1, b] = packed[t * span : (t + 1) * span]
        return 0

    lax.fori_loop(0, tiles, finish, 0)
    copies = [pltpu.make_async_copy(ys.at[k], outs[k], sems.at[k]) for k in range(n)]
    for copy in copies:
        copy.start()
    for copy in copies:
        copy.wait()


def attention(received, slots, tables, per_device):
    n = len(received)
    span = received[0].shape[2]
    blocks = n * per_device
    length = blocks * span
    big = span * (2 if blocks % 2 == 0 else 1)
    tiles = length // big
    anywhere = pl.BlockSpec(memory_space=pl.ANY)
    vmem = pl.BlockSpec(memory_space=pltpu.VMEM)
    pairs = tiles * (tiles + 1) // 2 * big * big
    turned = pltpu.VMEM((length, LANES), low)
    return pl.pallas_call(
        functools.partial(attention_kernel, n, per_device),
        in_specs=[pl.BlockSpec(memory_space=pltpu.SMEM)] + [anywhere] * n + [vmem] * 2,
        out_specs=[anywhere] * n,
        out_shape=[jax.ShapeDtypeStruct(received[0].shape, low)] * n,
        scratch_shapes=[
            pltpu.VMEM((n,) + received[0].shape, low),
            pltpu.VMEM((n,) + received[0].shape, low),
            turned,
            turned,
            turned,
            turned,
            pltpu.VMEM((tiles, HEAD_DIM, big), low),
            pltpu.VMEM((tiles, HEAD_DIM, big), low),
            pltpu.VMEM((tiles, big, big), wide),
            pltpu.VMEM((tiles, big, LANES), wide),
            pltpu.SemaphoreType.DMA((n,)),
        ],
        compiler_params=pltpu.CompilerParams(vmem_limit_bytes=40 * 2**20),
        cost_estimate=pl.CostEstimate(
            flops=12 * pairs * 512, bytes_accessed=8 * 2**20, transcendentals=pairs
        ),
    )(slots, *received, *tables)


def close_kernel(
    back, mix, proj, out, part, res, scale, both, attended_out, linear_out, sums, offs
):
    heads = back.shape[0]
    model = res.shape[2]
    normed = normalize_block(res[0].astype(wide))
    kinds = []
    for kind in range(2):
        kinds += unpack_heads([back[h, kind, 0].astype(wide) for h in range(heads)])
    attended, linear = kinds[0].astype(low), [x.astype(low) for x in kinds[1:]]
    attended_out[...] = attended
    both[:, :model] = (dot_nn(attended, mix[...]) + out[...]).astype(low)
    attn_part = sum(dot_nt(linear[i], proj[i]) for i in range(3))
    feed_part = part[...]
    both[:, model:] = (attn_part * scale[0:1] + feed_part * scale[1:2]).astype(low)

    @pl.when(pl.program_id(0) == 0)
    def _():
        sums[...] = jnp.zeros_like(sums)
        offs[...] = jnp.zeros_like(offs)

    for i in range(3):
        linear_out[i] = linear[i]
        offs[i : i + 1] += jnp.sum(kinds[1 + i].astype(low).astype(wide), axis=0, keepdims=True)
    for i, x in enumerate([attn_part * normed, feed_part * normed, attn_part, feed_part]):
        sums[i : i + 1] += jnp.sum(x, axis=0, keepdims=True)


def close(back, mixing, projections, out, part, residual, scale, first):
    heads, _, per_device, span, _ = back.shape
    local, model = mixing.shape
    whole = lambda *shape: pl.BlockSpec(shape, lambda t: (0,) * len(shape))
    rows = lambda columns: pl.BlockSpec((span, columns), lambda t: (t, 0))
    later = lambda columns: pl.BlockSpec((span, columns), lambda t: (first + t, 0))
    count = per_device * span
    return pl.pallas_call(
        close_kernel,
        grid=(per_device,),
        in_specs=[
            pl.BlockSpec((heads, 2, 1, span, LANES), lambda t: (0, 0, t, 0, 0)),
            whole(local, model),
            whole(3, model, local),
            later(model),
            later(model),
            pl.BlockSpec((1, span, model), lambda t: (first + t, 0, 0)),
            whole(2, model),
        ],
        out_specs=[
            rows(2 * model),
            rows(local),
            pl.BlockSpec((3, span, local), lambda t: (0, t, 0)),
            whole(8, model),
            whole(8, local),
        ],
        out_shape=[
            jax.ShapeDtypeStruct((count, 2 * model), low),
            jax.ShapeDtypeStruct((count, local), low),
            jax.ShapeDtypeStruct((3, count, local), low),
            jax.ShapeDtypeStruct((8, model), wide),
            jax.ShapeDtypeStruct((8, local), wide),
        ],
        compiler_params=pltpu.CompilerParams(vmem_limit_bytes=58 * 2**20),
        cost_estimate=pl.CostEstimate(
            flops=8 * count * model * local, bytes_accessed=12 * 2**20, transcendentals=0
        ),
    )(back, mixing, projections, out, part, residual, scale)


def steps_over(*axes):
    steps = []
    for axis in axes:
        size = lax.axis_size(axis)
        bit = 1
        while bit < size:
            steps.append((axis, [(s, s ^ bit) for s in range(size)], bit))
            bit *= 2
    return steps


def side_of(axis, bit):
    return (lax.axis_index(axis) // bit) % 2


class Order:
    def __init__(self):
        self.token = jnp.zeros((8, LANES), wide)

    def __call__(self, x):
        x, self.token = lax.optimization_barrier((x, self.token))
        return x


class RowSum:
    def __init__(self, x, steps, order, middle=lambda x: x):
        self.x, self.steps, self.order, self.middle = x, steps, order, middle
        self.at = 0

    def step(self):
        count = len(self.steps)
        if self.at < count:
            axis, perm, bit = self.steps[self.at]
            half = self.x.shape[0] // 2
            side = side_of(axis, bit)
            sent = lax.dynamic_slice_in_dim(self.x, (1 - side) * half, half, 0).astype(low)
            kept = lax.dynamic_slice_in_dim(self.x, side * half, half, 0)
            got = lax.ppermute(self.order(sent), axis, perm)
            self.x = kept.astype(wide) + got.astype(wide)
            if self.at == count - 1:
                self.x = self.middle(self.x).astype(low)
        elif self.at < 2 * count:
            axis, perm, bit = self.steps[2 * count - 1 - self.at]
            x = self.order(self.x)
            got = lax.ppermute(x, axis, perm)
            self.x = jnp.where(
                side_of(axis, bit) == 0,
                jnp.concatenate([x, got], axis=0),
                jnp.concatenate([got, x], axis=0),
            )
        self.at += 1

    def done(self):
        return self.at >= 2 * len(self.steps)


def own_rows(x, steps):
    for axis, _, bit in steps:
        half = x.shape[0] // 2
        x = lax.dynamic_slice_in_dim(x, side_of(axis, bit) * half, half, 0)
    return x


def sum_small(x, steps):
    for axis, perm, _ in steps:
        x = x + lax.ppermute(x, axis, perm)
    return x


def on_device(
    residual,
    block_order,
    projections,
    offsets,
    mixing,
    baseline,
    expand,
    thresholds,
    contract,
    norm_scale,
    norm_shift,
    cotangent,
):
    seq_count, local_rows, model = residual.shape
    local = mixing.shape[0]
    heads = local // HEAD_DIM
    n = lax.axis_size("seq")
    me = lax.axis_index("seq")
    blocks = block_order.shape[1]
    length = local_rows * n
    span = length // blocks
    per_device = blocks // n
    tokens = seq_count * local_rows
    rounds = seq_count * heads // n
    tables = [jnp.asarray(t) for t in rotary_tables(length)]
    order = Order()
    batch_steps = steps_over("dp", "seq")
    tensor_steps = steps_over("tensor")

    own_blocks = lax.dynamic_slice_in_dim(block_order, me * per_device, per_device, 1).reshape(-1)
    residual_blocks = residual.reshape(seq_count * per_device, span, model)
    sends, attn_in, feed_in = project(
        residual_blocks,
        cotangent.reshape(residual_blocks.shape),
        own_blocks,
        projections,
        offsets,
        mixing,
        norm_scale,
        norm_shift,
        tables,
        (seq_count, per_device, heads),
    )
    received = []
    for r in range(rounds):
        received.append([lax.dynamic_index_in_dim(sends, r * n + me, 0, keepdims=False)])
        for k in range(1, n):
            part = lax.dynamic_index_in_dim(sends, r * n + (me + k) % n, 0, keepdims=False)
            received[r].append(
                lax.ppermute(order(part), "seq", [(s, (s + k) % n) for s in range(n)])
            )

    stored = jnp.arange(blocks, dtype=jnp.int32)
    slot_of = ((me - stored // per_device) % n) * per_device + stored % per_device

    def slots_in(r):
        order = lax.dynamic_index_in_dim(block_order, (r * n + me) // heads, 0, keepdims=False)
        return jnp.sum(
            jnp.where(order[None, :] == stored[:, None], slot_of[None, :], 0), axis=1
        ).astype(jnp.int32)

    attn_in = attn_in.reshape(tokens, model)
    feed_in = order(feed_in).reshape(tokens, model)
    upstream_low = cotangent.reshape(tokens, model)
    activated, grad_hidden, feed_out, feed_part, feed_sums = feed_forward(
        feed_in, upstream_low, expand, thresholds, contract, span
    )

    def dot_tn(a, b):
        return lax.dot_general(a, b, (((0,), (0,)), ((), ())), preferred_element_type=wide)

    grad_contract, grad_expand = lax.psum(
        order((dot_tn(activated, upstream_low).astype(low), dot_tn(feed_in, grad_hidden).astype(low))),
        ("dp", "seq"),
    )

    back = []
    for r in range(rounds):
        pieces = attention(received[r], slots_in(r), tables, per_device)
        full = jnp.zeros((n,) + pieces[0].shape, low)
        for k in range(n):
            piece = pieces[k]
            if k:
                piece = lax.ppermute(
                    order(piece), "seq", [(s, (s - k) % n) for s in range(n)]
                )
            full = lax.dynamic_update_index_in_dim(full, piece, (me + k) % n, 0)
        back.append(full)

    flat_residual = residual.reshape(tokens, model)

    def finish(mine, totals):
        inputs = own_rows(flat_residual[mine], tensor_steps).astype(wide)
        layer_own = inputs + totals[:, :model] + baseline
        combined = totals[:, model:]
        centred = inputs - jnp.mean(inputs, axis=-1, keepdims=True)
        inverse = lax.rsqrt(jnp.mean(centred * centred, axis=-1, keepdims=True) + norm_eps)
        normed = centred * inverse
        grad_own = own_rows(upstream_low[mine], tensor_steps).astype(wide) + inverse * (
            combined
            - jnp.mean(combined, axis=-1, keepdims=True)
            - normed * jnp.mean(combined * normed, axis=-1, keepdims=True)
        )
        return jnp.concatenate([layer_own.astype(low), grad_own.astype(low)], axis=1)

    small_sums, branches, attended, grad_linear = [], [], [], []
    for s in range(seq_count):
        pairs = range(s * heads, (s + 1) * heads)
        if heads % n == 0:
            pieces = [back[r] for r in range(s * heads // n, (s + 1) * heads // n)]
            pairs_back = pieces[0] if len(pieces) == 1 else jnp.concatenate(pieces, axis=0)
        else:
            pairs_back = jnp.stack([back[p // n][p % n] for p in pairs])
        if s:
            pairs_back = order(pairs_back)
        both, attended_s, linear_s, sums_s, offs_s = close(
            pairs_back,
            mixing,
            projections,
            feed_out,
            feed_part,
            residual_blocks,
            norm_scale,
            s * per_device,
        )
        attended.append(attended_s)
        grad_linear.append(linear_s)
        small_sums.append((sums_s, offs_s))
        mine = slice(s * local_rows, (s + 1) * local_rows)
        branches.append(RowSum(both, tensor_steps, order, functools.partial(finish, mine)))
        branches[s].step()
        if s < seq_count - 1:
            branches[s].step()

    attended = jnp.concatenate(attended, axis=0)
    grad_linear = jnp.concatenate(grad_linear, axis=1)
    grad_projections = RowSum(
        jnp.concatenate([dot_tn(attn_in, grad_linear[i]) for i in range(3)], axis=0),
        batch_steps,
        order,
    )
    grad_projections.step()
    sums = sum_small(sum(s for s, _ in small_sums)[:4], tensor_steps)
    grad_offsets = sum(o for _, o in small_sums)[:3]
    small = jnp.concatenate(
        [sums.reshape(-1), grad_offsets.reshape(-1), feed_sums[0], feed_sums[1]]
    )
    shares = 1
    for axis, _, _ in batch_steps:
        shares *= 2
    unit = model * shares
    padded = -(-small.shape[0] // unit) * unit
    small_rows = jnp.pad(small, (0, padded - small.shape[0])).reshape(-1, model)
    grad_mixing = RowSum(
        jnp.concatenate([dot_tn(attended, upstream_low), small_rows], axis=0), batch_steps, order
    )
    grad_mixing.step()
    params = [grad_projections, grad_mixing]
    while not all(b.done() for b in branches + params):
        for chain in branches[::-1] + params:
            chain.step()

    results = jnp.stack([b.x for b in branches])
    grad_projections = grad_projections.x.astype(wide).reshape(3, model, local)
    small = grad_mixing.x[local:].astype(wide).reshape(-1)
    grad_mixing = grad_mixing.x[:local].astype(wide)
    grad_contract, grad_expand = grad_contract.astype(wide), grad_expand.astype(wide)
    sizes = [2 * model, 2 * model, 3 * local, thresholds.shape[0], model]
    cuts = np.cumsum(sizes)
    grad_scale, grad_shift, grad_offsets, grad_thresholds, grad_baseline = jnp.split(
        small[: cuts[-1]], cuts[:-1]
    )
    return (
        results[:, :, :model],
        results[:, :, model:],
        grad_projections,
        grad_offsets.reshape(3, local),
        grad_mixing,
        grad_baseline,
        grad_expand,
        grad_thresholds,
        grad_contract,
        grad_scale.reshape(2, model),
        grad_shift.reshape(2, model),
    )


def solution(mesh):
    in_specs = (
        P("dp", "seq", None),
        P("dp", None),
        P(None, None, "tensor"),
        P(None, "tensor"),
        P("tensor", None),
        P(),
        P(None, "tensor"),
        P("tensor"),
        P("tensor", None),
        P(),
        P(),
        P("dp", "seq", None),
    )
    out_specs = (
        P("dp", "seq", None),
        P("dp", "seq", None),
        P(None, None, "tensor"),
        P(None, "tensor"),
        P("tensor", None),
        P(),
        P(None, "tensor"),
        P("tensor"),
        P("tensor", None),
        P(),
        P(),
    )
    return jax.shard_map(
        on_device, mesh=mesh, in_specs=in_specs, out_specs=out_specs, check_vma=False
    )
```

```python
import functools

import jax
import jax.numpy as jnp
import numpy as np
from jax import lax
from jax.experimental import pallas as pl
from jax.experimental.pallas import tpu as pltpu
from jax.sharding import PartitionSpec as P

HEAD_DIM = 64
ROT = 16
LANES = 128

norm_eps = 1e-05
masked_value = -1e30
low = jnp.bfloat16
wide = jnp.float32


def dot_nn(a, b):
    return lax.dot_general(a, b, (((1,), (0,)), ((), ())), preferred_element_type=wide)


def dot_nt(a, b):
    return lax.dot_general(a, b, (((1,), (1,)), ((), ())), preferred_element_type=wide)


def rotary_tables(length):
    half = ROT // 2
    freqs = np.float32(10000.0) ** (-np.arange(half, dtype=np.float32) * 2.0 / ROT)
    angles = np.arange(length, dtype=np.float32)[:, None] * freqs.astype(np.float32)
    cosine = np.ones((length, HEAD_DIM), np.float32)
    sine = np.zeros((length, HEAD_DIM), np.float32)
    cosine[:, :half] = np.cos(angles)
    cosine[:, half:ROT] = np.cos(angles)
    sine[:, :half] = -np.sin(angles)
    sine[:, half:ROT] = np.sin(angles)
    return np.tile(cosine, (1, LANES // HEAD_DIM)), np.tile(sine, (1, LANES // HEAD_DIM))


def rotate_lanes(x, cosine, sine):
    width = x.shape[1]
    if width < LANES:
        x = jnp.concatenate([x, x], axis=1)
    lane = lax.broadcasted_iota(jnp.int32, x.shape, 1) % HEAD_DIM
    partner = jnp.where(
        lane < ROT // 2, pltpu.roll(x, LANES - ROT // 2, 1), pltpu.roll(x, ROT // 2, 1)
    )
    return (x * cosine + partner * sine)[:, :width]


def half_lanes(shape):
    return lax.broadcasted_iota(jnp.int32, shape, 1) < HEAD_DIM


def swap_halves(x):
    return pltpu.roll(x, HEAD_DIM, 1)


def pack_heads(first, second):
    packed = []
    for c in range(0, first.shape[1], LANES):
        x, y = first[:, c : c + LANES], second[:, c : c + LANES]
        lower = half_lanes(x.shape)
        packed.append(jnp.where(lower, x, swap_halves(y)))
        packed.append(jnp.where(lower, swap_halves(x), y))
    return packed


def unpack_heads(packed):
    first, second = [], []
    for h in range(0, len(packed), 2):
        x, y = packed[h], packed[h + 1]
        lower = half_lanes(x.shape)
        first.append(jnp.where(lower, x, swap_halves(y)))
        second.append(jnp.where(lower, swap_halves(x), y))
    return jnp.concatenate(first, axis=1), jnp.concatenate(second, axis=1)


def normalize_block(x):
    centred = x - jnp.mean(x, axis=1, keepdims=True)
    inverse = lax.rsqrt(jnp.mean(centred * centred, axis=1, keepdims=True) + norm_eps)
    return centred * inverse


def project_kernel(
    places, res, cot, proj, offs, mix, scale, shift, cosine, sine, out, attn_out, feed_out
):
    normed = normalize_block(res[0].astype(wide))
    attn_in = (normed * scale[0:1] + shift[0:1]).astype(low)
    attn_out[0] = attn_in
    feed_out[0] = (normed * scale[1:2] + shift[1:2]).astype(low)
    rows = []
    for i in range(3):
        linear = dot_nn(attn_in, proj[i]) + offs[i : i + 1]
        if i < 2:
            linear = jnp.concatenate(
                [
                    rotate_lanes(linear[:, c : c + LANES], cosine[...], sine[...])
                    for c in range(0, linear.shape[1], LANES)
                ],
                axis=1,
            )
        rows.append(linear)
    rows.append(dot_nt(cot[0], mix[...]))
    for kind in range(2):
        for h, x in enumerate(pack_heads(rows[2 * kind], rows[2 * kind + 1])):
            out[h, kind, 0] = x.astype(low)


def project(residual, cotangent, places, projections, offsets, mixing, scale, shift, tables, dims):
    blocks, span, model = residual.shape
    seq_count, per_device, heads = dims
    local = projections.shape[2]
    whole = lambda *shape: pl.BlockSpec(shape, lambda t, p: (0,) * len(shape))
    token = pl.BlockSpec((1, span, model), lambda t, p: (t, 0, 0))
    table = pl.BlockSpec((span, LANES), lambda t, p: (p[t], 0))
    return pl.pallas_call(
        project_kernel,
        grid_spec=pltpu.PrefetchScalarGridSpec(
            num_scalar_prefetch=1,
            grid=(blocks,),
            in_specs=[
                token,
                token,
                whole(3, model, local),
                whole(3, local),
                whole(local, model),
                whole(2, model),
                whole(2, model),
                table,
                table,
            ],
            out_specs=[
                pl.BlockSpec(
                    (heads, 2, 1, span, LANES),
                    lambda t, p: (t // per_device, 0, t % per_device, 0, 0),
                ),
                token,
                token,
            ],
        ),
        out_shape=[
            jax.ShapeDtypeStruct((seq_count * heads, 2, per_device, span, LANES), low),
            jax.ShapeDtypeStruct((blocks, span, model), low),
            jax.ShapeDtypeStruct((blocks, span, model), low),
        ],
        compiler_params=pltpu.CompilerParams(vmem_limit_bytes=58 * 2**20),
        cost_estimate=pl.CostEstimate(
            flops=8 * blocks * span * model * local, bytes_accessed=12 * 2**20, transcendentals=0
        ),
    )(places, residual, cotangent, projections, offsets, mixing, scale, shift, *tables)


def feed_kernel(feed, cot, expand, thresholds, contract, act, grad, out, part, sums):
    hidden = dot_nn(feed[...], expand[...]) + thresholds[...]
    normal = 0.5 + 0.5 * lax.erf(hidden * float(np.sqrt(0.5)))
    density = jnp.exp(-0.5 * hidden * hidden) * float(1.0 / np.sqrt(2.0 * np.pi))
    activated = (hidden * normal).astype(low)
    act[...] = activated
    slope = normal + hidden * density
    grad_hidden = (dot_nt(cot[...], contract[...]) * slope).astype(low)
    grad[...] = grad_hidden
    out[...] = dot_nn(activated, contract[...])
    part[...] = dot_nt(grad_hidden, expand[...])

    @pl.when(pl.program_id(0) == 0)
    def _():
        sums[...] = jnp.zeros_like(sums)

    sums[0:1] += jnp.sum(grad_hidden.astype(wide), axis=0, keepdims=True)
    sums[1:2] += jnp.sum(cot[...].astype(wide), axis=0, keepdims=True)


def feed_forward(feed_in, upstream, expand, thresholds, contract, span):
    tokens, model = feed_in.shape
    units = expand.shape[1]
    whole = lambda *shape: pl.BlockSpec(shape, lambda t: (0,) * len(shape))
    rows = lambda columns: pl.BlockSpec((span, columns), lambda t: (t, 0))
    return pl.pallas_call(
        feed_kernel,
        grid=(tokens // span,),
        in_specs=[
            rows(model),
            rows(model),
            whole(model, units),
            whole(1, units),
            whole(units, model),
        ],
        out_specs=[rows(units), rows(units), rows(model), rows(model), whole(8, units)],
        out_shape=[
            jax.ShapeDtypeStruct((tokens, units), low),
            jax.ShapeDtypeStruct((tokens, units), low),
            jax.ShapeDtypeStruct((tokens, model), wide),
            jax.ShapeDtypeStruct((tokens, model), wide),
            jax.ShapeDtypeStruct((8, units), wide),
        ],
        compiler_params=pltpu.CompilerParams(vmem_limit_bytes=58 * 2**20),
        cost_estimate=pl.CostEstimate(
            flops=8 * tokens * model * units,
            bytes_accessed=20 * 2**20,
            transcendentals=2 * tokens * units,
        ),
    )(feed_in, upstream, expand, thresholds.reshape(1, units), contract)


def attention_kernel(n, per_device, slots, *refs):
    received, refs = refs[:n], refs[n:]
    cosine, sine = refs[0], refs[1]
    outs, refs = refs[2 : 2 + n], refs[2 + n :]
    xs, ys, k_lo, q_lo, v_hi, g_hi, k_turned, v_turned, strip, sums, sems = refs
    blocks = n * per_device
    span = xs.shape[3]
    tiles, big = strip.shape[0], strip.shape[1]
    ratio = big // span
    scale = HEAD_DIM ** (-0.5)
    to_log2 = scale * float(np.log2(np.e))

    copies = [pltpu.make_async_copy(received[k], xs.at[k], sems.at[k]) for k in range(n)]
    for copy in copies:
        copy.start()
    sums[...] = jnp.zeros_like(sums)
    for copy in copies:
        copy.wait()

    def place(j):
        slot = slots[j]
        return slot // per_device, slot % per_device

    def rows_of(u, size):
        return pl.ds(pl.multiple_of(u * size, size), size)

    lower = half_lanes((span, LANES))

    def order(j, _):
        a, b = place(j)
        rows = rows_of(j, span)
        x, y = xs[a, 0, b].astype(wide), xs[a, 1, b].astype(wide)
        k_lo[rows] = swap_halves(x).astype(low)
        q_lo[rows] = jnp.where(lower, x, 0.0).astype(low)
        v_hi[rows] = swap_halves(y).astype(low)
        g_hi[rows] = jnp.where(lower, 0.0, y).astype(low)
        return 0

    lax.fori_loop(0, blocks, order, 0)

    def turn(u, _):
        rows = rows_of(u, big)
        k_turned[u] = k_lo[rows].astype(wide).T[:HEAD_DIM].astype(low)
        v_turned[u] = v_hi[rows].astype(wide).T[HEAD_DIM:].astype(low)
        return 0

    lax.fori_loop(0, tiles, turn, 0)
    allowed = lax.broadcasted_iota(jnp.int32, (big, big), 0) <= lax.broadcasted_iota(
        jnp.int32, (big, big), 1
    )
    lower_big = half_lanes((big, LANES))

    def query_tile(u, _):
        own = rows_of(u, big)
        q, g = q_lo[own], g_hi[own]
        g_turned = g.astype(wide).T[HEAD_DIM:]

        s = jnp.where(allowed, dot_nt(k_lo[own], q), masked_value)
        strip[u] = s
        top = jnp.max(s, axis=0, keepdims=True)

        def scores(j, top):
            s = dot_nt(k_lo[rows_of(j, big)], q)
            strip[j] = s
            return jnp.maximum(top, jnp.max(s, axis=0, keepdims=True))

        top = lax.fori_loop(0, u, scores, top)

        def weigh(j, carry):
            total, out = carry
            p = jnp.exp2((strip[j] - top) * to_log2)
            strip[j] = p
            return total + jnp.sum(p, axis=0, keepdims=True), out + dot_nn(
                v_turned[j], p.astype(low)
            )

        zeros = jnp.zeros((HEAD_DIM, big), wide)
        total, out = lax.fori_loop(0, u + 1, weigh, (jnp.zeros((1, big), wide), zeros))
        recip = 1.0 / total
        out = out * recip
        slope_scale = scale * recip
        slope_shift = slope_scale * jnp.sum(out * g_turned, axis=0, keepdims=True)

        def back(j, dq):
            p = strip[j]
            dots = dot_nt(v_hi[rows_of(j, big)], g)
            slopes = (p * (dots * slope_scale - slope_shift)).astype(low)
            sums[j] += dot_nn(slopes, q) + dot_nn((p * recip).astype(low), g)
            return dq + dot_nn(k_turned[j], slopes)

        dq = lax.fori_loop(0, u + 1, back, zeros)
        packed = jnp.concatenate([out, dq], axis=0).T
        packed = jnp.where(lower_big, packed, rotate_lanes(packed, cosine[own], -sine[own]))
        packed = packed.astype(low)
        for t in range(ratio):
            a, b = place(u * ratio + t)
            ys[a, 0, b] = packed[t * span : (t + 1) * span]
        return 0

    lax.fori_loop(0, tiles, query_tile, 0)

    def finish(u, _):
        own = rows_of(u, big)
        x = sums[u]
        packed = jnp.where(lower_big, rotate_lanes(x, cosine[own], -sine[own]), x).astype(low)
        for t in range(ratio):
            a, b = place(u * ratio + t)
            ys[a, 1, b] = packed[t * span : (t + 1) * span]
        return 0

    lax.fori_loop(0, tiles, finish, 0)
    copies = [pltpu.make_async_copy(ys.at[k], outs[k], sems.at[k]) for k in range(n)]
    for copy in copies:
        copy.start()
    for copy in copies:
        copy.wait()


def attention(received, slots, tables, per_device):
    n = len(received)
    span = received[0].shape[2]
    blocks = n * per_device
    length = blocks * span
    big = span * (2 if blocks % 2 == 0 else 1)
    tiles = length // big
    anywhere = pl.BlockSpec(memory_space=pl.ANY)
    vmem = pl.BlockSpec(memory_space=pltpu.VMEM)
    pairs = tiles * (tiles + 1) // 2 * big * big
    turned = pltpu.VMEM((length, LANES), low)
    return pl.pallas_call(
        functools.partial(attention_kernel, n, per_device),
        in_specs=[pl.BlockSpec(memory_space=pltpu.SMEM)] + [anywhere] * n + [vmem] * 2,
        out_specs=[anywhere] * n,
        out_shape=[jax.ShapeDtypeStruct(received[0].shape, low)] * n,
        scratch_shapes=[
            pltpu.VMEM((n,) + received[0].shape, low),
            pltpu.VMEM((n,) + received[0].shape, low),
            turned,
            turned,
            turned,
            turned,
            pltpu.VMEM((tiles, HEAD_DIM, big), low),
            pltpu.VMEM((tiles, HEAD_DIM, big), low),
            pltpu.VMEM((tiles, big, big), wide),
            pltpu.VMEM((tiles, big, LANES), wide),
            pltpu.SemaphoreType.DMA((n,)),
        ],
        compiler_params=pltpu.CompilerParams(vmem_limit_bytes=40 * 2**20),
        cost_estimate=pl.CostEstimate(
            flops=12 * pairs * 512, bytes_accessed=8 * 2**20, transcendentals=pairs
        ),
    )(slots, *received, *tables)


def close_kernel(
    back, mix, proj, out, part, res, scale, both, attended_out, linear_out, sums, offs
):
    heads = back.shape[0]
    model = res.shape[2]
    normed = normalize_block(res[0].astype(wide))
    kinds = []
    for kind in range(2):
        kinds += unpack_heads([back[h, kind, 0].astype(wide) for h in range(heads)])
    attended, linear = kinds[0].astype(low), [x.astype(low) for x in kinds[1:]]
    attended_out[...] = attended
    both[:, :model] = (dot_nn(attended, mix[...]) + out[...]).astype(low)
    attn_part = sum(dot_nt(linear[i], proj[i]) for i in range(3))
    feed_part = part[...]
    both[:, model:] = (attn_part * scale[0:1] + feed_part * scale[1:2]).astype(low)

    @pl.when(pl.program_id(0) == 0)
    def _():
        sums[...] = jnp.zeros_like(sums)
        offs[...] = jnp.zeros_like(offs)

    for i in range(3):
        linear_out[i] = linear[i]
        offs[i : i + 1] += jnp.sum(kinds[1 + i].astype(low).astype(wide), axis=0, keepdims=True)
    for i, x in enumerate([attn_part * normed, feed_part * normed, attn_part, feed_part]):
        sums[i : i + 1] += jnp.sum(x, axis=0, keepdims=True)


def close(back, mixing, projections, out, part, residual, scale, first):
    heads, _, per_device, span, _ = back.shape
    local, model = mixing.shape
    whole = lambda *shape: pl.BlockSpec(shape, lambda t: (0,) * len(shape))
    rows = lambda columns: pl.BlockSpec((span, columns), lambda t: (t, 0))
    later = lambda columns: pl.BlockSpec((span, columns), lambda t: (first + t, 0))
    count = per_device * span
    return pl.pallas_call(
        close_kernel,
        grid=(per_device,),
        in_specs=[
            pl.BlockSpec((heads, 2, 1, span, LANES), lambda t: (0, 0, t, 0, 0)),
            whole(local, model),
            whole(3, model, local),
            later(model),
            later(model),
            pl.BlockSpec((1, span, model), lambda t: (first + t, 0, 0)),
            whole(2, model),
        ],
        out_specs=[
            rows(2 * model),
            rows(local),
            pl.BlockSpec((3, span, local), lambda t: (0, t, 0)),
            whole(8, model),
            whole(8, local),
        ],
        out_shape=[
            jax.ShapeDtypeStruct((count, 2 * model), low),
            jax.ShapeDtypeStruct((count, local), low),
            jax.ShapeDtypeStruct((3, count, local), low),
            jax.ShapeDtypeStruct((8, model), wide),
            jax.ShapeDtypeStruct((8, local), wide),
        ],
        compiler_params=pltpu.CompilerParams(vmem_limit_bytes=58 * 2**20),
        cost_estimate=pl.CostEstimate(
            flops=8 * count * model * local, bytes_accessed=12 * 2**20, transcendentals=0
        ),
    )(back, mixing, projections, out, part, residual, scale)


def steps_over(*axes):
    steps = []
    for axis in axes:
        size = lax.axis_size(axis)
        bit = 1
        while bit < size:
            steps.append((axis, [(s, s ^ bit) for s in range(size)], bit))
            bit *= 2
    return steps


def side_of(axis, bit):
    return (lax.axis_index(axis) // bit) % 2


def after(x, earlier):
    first = earlier[(0,) * earlier.ndim].astype(wide)
    return x + jnp.minimum(jnp.abs(first), 0.0).astype(x.dtype)


class RowSum:
    def __init__(self, x, steps, middle=lambda x: x):
        self.x, self.steps, self.middle = x, steps, middle
        self.sent = None
        self.at = 0

    def step(self, earlier=None):
        count = len(self.steps)
        if self.done():
            return
        if self.at < count:
            axis, perm, bit = self.steps[self.at]
            half = self.x.shape[0] // 2
            side = side_of(axis, bit)
            sent = lax.dynamic_slice_in_dim(self.x, (1 - side) * half, half, 0).astype(low)
            kept = lax.dynamic_slice_in_dim(self.x, side * half, half, 0)
            if earlier is not None:
                sent = after(sent, earlier)
            self.sent = sent
            got = lax.ppermute(sent, axis, perm)
            self.x = kept.astype(wide) + got.astype(wide)
            if self.at == count - 1:
                self.x = self.middle(self.x).astype(low)
        else:
            axis, perm, bit = self.steps[2 * count - 1 - self.at]
            x = self.x if earlier is None else after(self.x, earlier)
            self.sent = x
            got = lax.ppermute(x, axis, perm)
            self.last = (side_of(axis, bit), x, got)
            self.x = jnp.where(
                side_of(axis, bit) == 0,
                jnp.concatenate([x, got], axis=0),
                jnp.concatenate([got, x], axis=0),
            )
        self.at += 1

    def done(self):
        return self.at >= 2 * len(self.steps)


def own_rows(x, steps):
    for axis, _, bit in steps:
        half = x.shape[0] // 2
        x = lax.dynamic_slice_in_dim(x, side_of(axis, bit) * half, half, 0)
    return x


def sum_small(x, steps):
    for axis, perm, _ in steps:
        x = x + lax.ppermute(x, axis, perm)
    return x


def on_device(
    residual,
    block_order,
    projections,
    offsets,
    mixing,
    baseline,
    expand,
    thresholds,
    contract,
    norm_scale,
    norm_shift,
    cotangent,
):
    seq_count, local_rows, model = residual.shape
    local = mixing.shape[0]
    heads = local // HEAD_DIM
    n = lax.axis_size("seq")
    me = lax.axis_index("seq")
    blocks = block_order.shape[1]
    length = local_rows * n
    span = length // blocks
    per_device = blocks // n
    tokens = seq_count * local_rows
    rounds = seq_count * heads // n
    tables = [jnp.asarray(t) for t in rotary_tables(length)]
    batch_steps = steps_over("dp", "seq")
    tensor_steps = steps_over("tensor")

    own_blocks = lax.dynamic_slice_in_dim(block_order, me * per_device, per_device, 1).reshape(-1)
    residual_blocks = residual.reshape(seq_count * per_device, span, model)
    sends, attn_in, feed_in = project(
        residual_blocks,
        cotangent.reshape(residual_blocks.shape),
        own_blocks,
        projections,
        offsets,
        mixing,
        norm_scale,
        norm_shift,
        tables,
        (seq_count, per_device, heads),
    )
    received = []
    for r in range(rounds):
        first = r * n
        received.append([lax.dynamic_index_in_dim(sends, r * n + me, 0, keepdims=False)])
        for k in range(1, n):
            part = lax.dynamic_index_in_dim(sends, first + (me + k) % n, 0, keepdims=False)
            received[r].append(lax.ppermute(part, "seq", [(s, (s + k) % n) for s in range(n)]))

    stored = jnp.arange(blocks, dtype=jnp.int32)
    slot_of = ((me - stored // per_device) % n) * per_device + stored % per_device

    def slots_in(r):
        order = lax.dynamic_index_in_dim(block_order, (r * n + me) // heads, 0, keepdims=False)
        return jnp.sum(
            jnp.where(order[None, :] == stored[:, None], slot_of[None, :], 0), axis=1
        ).astype(jnp.int32)

    attn_in = attn_in.reshape(tokens, model)
    feed_in = feed_in.reshape(tokens, model)
    upstream_low = cotangent.reshape(tokens, model)
    activated, grad_hidden, feed_out, feed_part, feed_sums = feed_forward(
        feed_in, upstream_low, expand, thresholds, contract, span
    )

    def dot_tn(a, b):
        return lax.dot_general(a, b, (((0,), (0,)), ((), ())), preferred_element_type=wide)

    grad_contract = lax.psum(dot_tn(activated, upstream_low).astype(low), ("dp", "seq"))
    expand_sum = RowSum(
        dot_tn(feed_in, grad_hidden),
        steps_over("dp"),
        lambda x: lax.psum(x.astype(low), "seq"),
    )
    for _ in expand_sum.steps:
        expand_sum.step()

    back = []
    for r in range(rounds):
        pieces = attention(received[r], slots_in(r), tables, per_device)
        full = jnp.zeros((n,) + pieces[0].shape, low)
        for k in range(n):
            piece = pieces[k]
            if k:
                piece = lax.ppermute(piece, "seq", [(s, (s - k) % n) for s in range(n)])
            full = lax.dynamic_update_index_in_dim(full, piece, (me + k) % n, 0)
        back.append(full)

    flat_residual = residual.reshape(tokens, model)

    def finish(mine, totals):
        inputs = own_rows(flat_residual[mine], tensor_steps).astype(wide)
        layer_own = inputs + totals[:, :model] + baseline
        combined = totals[:, model:]
        centred = inputs - jnp.mean(inputs, axis=-1, keepdims=True)
        inverse = lax.rsqrt(jnp.mean(centred * centred, axis=-1, keepdims=True) + norm_eps)
        normed = centred * inverse
        grad_own = own_rows(upstream_low[mine], tensor_steps).astype(wide) + inverse * (
            combined
            - jnp.mean(combined, axis=-1, keepdims=True)
            - normed * jnp.mean(combined * normed, axis=-1, keepdims=True)
        )
        return jnp.concatenate([layer_own.astype(low), grad_own.astype(low)], axis=1)

    small_sums, branches, attended, grad_linear = [], [], [], []
    for s in range(seq_count):
        pairs = range(s * heads, (s + 1) * heads)
        if heads % n == 0:
            pieces = [back[r] for r in range(s * heads // n, (s + 1) * heads // n)]
            pairs_back = pieces[0] if len(pieces) == 1 else jnp.concatenate(pieces, axis=0)
        else:
            pairs_back = jnp.stack([back[p // n][p % n] for p in pairs])
        both, attended_s, linear_s, sums_s, offs_s = close(
            pairs_back,
            mixing,
            projections,
            feed_out,
            feed_part,
            residual_blocks,
            after(norm_scale, branches[-1].sent) if branches else norm_scale,
            s * per_device,
        )
        attended.append(attended_s)
        grad_linear.append(linear_s)
        small_sums.append((sums_s, offs_s))
        mine = slice(s * local_rows, (s + 1) * local_rows)
        branches.append(RowSum(both, tensor_steps, functools.partial(finish, mine)))
        branches[s].step()
        if s < seq_count - 1:
            branches[s].step()

    attended = jnp.concatenate(attended, axis=0)
    grad_linear = jnp.concatenate(grad_linear, axis=1)
    sums = sum_small(sum(s for s, _ in small_sums)[:4], tensor_steps)
    grad_offsets = sum(o for _, o in small_sums)[:3]
    small = jnp.concatenate(
        [sums.reshape(-1), grad_offsets.reshape(-1), feed_sums[0], feed_sums[1]]
    )
    shares = 1
    for _ in batch_steps:
        shares *= 2
    unit = model * shares
    padded = -(-small.shape[0] // unit) * unit
    small_rows = jnp.pad(small, (0, padded - small.shape[0])).reshape(-1, model)
    params = [
        RowSum(
            jnp.concatenate([dot_tn(attn_in, grad_linear[i]) for i in range(3)], axis=0),
            batch_steps,
        ),
        RowSum(
            jnp.concatenate([dot_tn(attended, upstream_low), small_rows], axis=0), batch_steps
        ),
    ]
    params[0].step()
    params[1].step(params[0].sent)
    grad_contract = grad_contract.astype(wide)
    turn = 0
    while not all(b.done() for b in branches + params + [expand_sum]):
        for chain in branches[::-1]:
            chain.step()
        last = params[0].at == 2 * len(batch_steps) - 1
        params[0].step(grad_contract if last else expand_sum.sent if turn > 1 else None)
        if not params[1].done():
            params[1].step(params[0].sent)
        turn += 1
        if turn > 1:
            expand_sum.step(params[0].sent)
    grad_expand = expand_sum.x.astype(wide)

    layer_output = jnp.zeros((seq_count, local_rows, model), low)
    grad_residual = layer_output
    for s, chain in enumerate(branches):
        side, *pieces = chain.last
        for position, piece in zip((side, 1 - side), pieces):
            at = (s, position * piece.shape[0], 0)
            layer_output = lax.dynamic_update_slice(layer_output, piece[None, :, :model], at)
            grad_residual = lax.dynamic_update_slice(grad_residual, piece[None, :, model:], at)
    grad_projections = params[0].x.astype(wide).reshape(3, model, local)
    small = params[1].x[local:].astype(wide).reshape(-1)
    grad_mixing = params[1].x[:local].astype(wide)
    sizes = [2 * model, 2 * model, 3 * local, thresholds.shape[0], model]
    cuts = np.cumsum(sizes)
    grad_scale, grad_shift, grad_offsets, grad_thresholds, grad_baseline = jnp.split(
        small[: cuts[-1]], cuts[:-1]
    )
    return (
        layer_output,
        grad_residual,
        grad_projections,
        grad_offsets.reshape(3, local),
        grad_mixing,
        grad_baseline,
        grad_expand,
        grad_thresholds,
        grad_contract,
        grad_scale.reshape(2, model),
        grad_shift.reshape(2, model),
    )


def solution(mesh):
    in_specs = (
        P("dp", "seq", None),
        P("dp", None),
        P(None, None, "tensor"),
        P(None, "tensor"),
        P("tensor", None),
        P(),
        P(None, "tensor"),
        P("tensor"),
        P("tensor", None),
        P(),
        P(),
        P("dp", "seq", None),
    )
    out_specs = (
        P("dp", "seq", None),
        P("dp", "seq", None),
        P(None, None, "tensor"),
        P(None, "tensor"),
        P("tensor", None),
        P(),
        P(None, "tensor"),
        P("tensor"),
        P("tensor", None),
        P(),
        P(),
    )
    return jax.shard_map(
        on_device, mesh=mesh, in_specs=in_specs, out_specs=out_specs, check_vma=False
    )
```

```python
import functools

import jax
import jax.numpy as jnp
import numpy as np
from jax import lax
from jax.experimental import pallas as pl
from jax.experimental.pallas import tpu as pltpu
from jax.sharding import PartitionSpec as P

HEAD_DIM = 64
ROT = 16
LANES = 128

norm_eps = 1e-05
masked_value = -1e30
low = jnp.bfloat16
wide = jnp.float32


def dot_nn(a, b):
    return lax.dot_general(a, b, (((1,), (0,)), ((), ())), preferred_element_type=wide)


def dot_nt(a, b):
    return lax.dot_general(a, b, (((1,), (1,)), ((), ())), preferred_element_type=wide)


def rotary_tables(length):
    half = ROT // 2
    freqs = np.float32(10000.0) ** (-np.arange(half, dtype=np.float32) * 2.0 / ROT)
    angles = np.arange(length, dtype=np.float32)[:, None] * freqs.astype(np.float32)
    cosine = np.ones((length, HEAD_DIM), np.float32)
    sine = np.zeros((length, HEAD_DIM), np.float32)
    cosine[:, :half] = np.cos(angles)
    cosine[:, half:ROT] = np.cos(angles)
    sine[:, :half] = -np.sin(angles)
    sine[:, half:ROT] = np.sin(angles)
    return np.tile(cosine, (1, LANES // HEAD_DIM)), np.tile(sine, (1, LANES // HEAD_DIM))


def rotate_lanes(x, cosine, sine):
    width = x.shape[1]
    if width < LANES:
        x = jnp.concatenate([x, x], axis=1)
    lane = lax.broadcasted_iota(jnp.int32, x.shape, 1) % HEAD_DIM
    partner = jnp.where(
        lane < ROT // 2, pltpu.roll(x, LANES - ROT // 2, 1), pltpu.roll(x, ROT // 2, 1)
    )
    return (x * cosine + partner * sine)[:, :width]


def half_lanes(shape):
    return lax.broadcasted_iota(jnp.int32, shape, 1) < HEAD_DIM


def swap_halves(x):
    return pltpu.roll(x, HEAD_DIM, 1)


def pack_heads(first, second):
    packed = []
    for c in range(0, first.shape[1], LANES):
        x, y = first[:, c : c + LANES], second[:, c : c + LANES]
        lower = half_lanes(x.shape)
        packed.append(jnp.where(lower, x, swap_halves(y)))
        packed.append(jnp.where(lower, swap_halves(x), y))
    return packed


def unpack_heads(packed):
    first, second = [], []
    for h in range(0, len(packed), 2):
        x, y = packed[h], packed[h + 1]
        lower = half_lanes(x.shape)
        first.append(jnp.where(lower, x, swap_halves(y)))
        second.append(jnp.where(lower, swap_halves(x), y))
    return jnp.concatenate(first, axis=1), jnp.concatenate(second, axis=1)


def normalize_block(x):
    centred = x - jnp.mean(x, axis=1, keepdims=True)
    inverse = lax.rsqrt(jnp.mean(centred * centred, axis=1, keepdims=True) + norm_eps)
    return centred * inverse


def project_kernel(
    places, res, cot, proj, offs, mix, scale, shift, cosine, sine, out, attn_out, feed_out
):
    normed = normalize_block(res[0].astype(wide))
    attn_in = (normed * scale[0:1] + shift[0:1]).astype(low)
    attn_out[0] = attn_in
    feed_out[0] = (normed * scale[1:2] + shift[1:2]).astype(low)
    rows = []
    for i in range(3):
        linear = dot_nn(attn_in, proj[i]) + offs[i : i + 1]
        if i < 2:
            linear = jnp.concatenate(
                [
                    rotate_lanes(linear[:, c : c + LANES], cosine[...], sine[...])
                    for c in range(0, linear.shape[1], LANES)
                ],
                axis=1,
            )
        rows.append(linear)
    rows.append(dot_nt(cot[0], mix[...]))
    for kind in range(2):
        for h, x in enumerate(pack_heads(rows[2 * kind], rows[2 * kind + 1])):
            out[h, kind, 0] = x.astype(low)


def project(residual, cotangent, places, projections, offsets, mixing, scale, shift, tables, dims):
    blocks, span, model = residual.shape
    seq_count, per_device, heads = dims
    local = projections.shape[2]
    whole = lambda *shape: pl.BlockSpec(shape, lambda t, p: (0,) * len(shape))
    token = pl.BlockSpec((1, span, model), lambda t, p: (t, 0, 0))
    table = pl.BlockSpec((span, LANES), lambda t, p: (p[t], 0))
    return pl.pallas_call(
        project_kernel,
        grid_spec=pltpu.PrefetchScalarGridSpec(
            num_scalar_prefetch=1,
            grid=(blocks,),
            in_specs=[
                token,
                token,
                whole(3, model, local),
                whole(3, local),
                whole(local, model),
                whole(2, model),
                whole(2, model),
                table,
                table,
            ],
            out_specs=[
                pl.BlockSpec(
                    (heads, 2, 1, span, LANES),
                    lambda t, p: (t // per_device, 0, t % per_device, 0, 0),
                ),
                token,
                token,
            ],
        ),
        out_shape=[
            jax.ShapeDtypeStruct((seq_count * heads, 2, per_device, span, LANES), low),
            jax.ShapeDtypeStruct((blocks, span, model), low),
            jax.ShapeDtypeStruct((blocks, span, model), low),
        ],
        compiler_params=pltpu.CompilerParams(vmem_limit_bytes=58 * 2**20),
        cost_estimate=pl.CostEstimate(
            flops=8 * blocks * span * model * local, bytes_accessed=12 * 2**20, transcendentals=0
        ),
    )(places, residual, cotangent, projections, offsets, mixing, scale, shift, *tables)


def feed_kernel(feed, cot, expand, thresholds, contract, act, grad, out, part, sums):
    hidden = dot_nn(feed[...], expand[...]) + thresholds[...]
    normal = 0.5 + 0.5 * lax.erf(hidden * float(np.sqrt(0.5)))
    density = jnp.exp(-0.5 * hidden * hidden) * float(1.0 / np.sqrt(2.0 * np.pi))
    activated = (hidden * normal).astype(low)
    act[...] = activated
    slope = normal + hidden * density
    grad_hidden = (dot_nt(cot[...], contract[...]) * slope).astype(low)
    grad[...] = grad_hidden
    out[...] = dot_nn(activated, contract[...])
    part[...] = dot_nt(grad_hidden, expand[...])

    @pl.when(pl.program_id(0) == 0)
    def _():
        sums[...] = jnp.zeros_like(sums)

    sums[0:1] += jnp.sum(grad_hidden.astype(wide), axis=0, keepdims=True)
    sums[1:2] += jnp.sum(cot[...].astype(wide), axis=0, keepdims=True)


def feed_forward(feed_in, upstream, expand, thresholds, contract, span):
    tokens, model = feed_in.shape
    units = expand.shape[1]
    whole = lambda *shape: pl.BlockSpec(shape, lambda t: (0,) * len(shape))
    rows = lambda columns: pl.BlockSpec((span, columns), lambda t: (t, 0))
    return pl.pallas_call(
        feed_kernel,
        grid=(tokens // span,),
        in_specs=[
            rows(model),
            rows(model),
            whole(model, units),
            whole(1, units),
            whole(units, model),
        ],
        out_specs=[rows(units), rows(units), rows(model), rows(model), whole(8, units)],
        out_shape=[
            jax.ShapeDtypeStruct((tokens, units), low),
            jax.ShapeDtypeStruct((tokens, units), low),
            jax.ShapeDtypeStruct((tokens, model), wide),
            jax.ShapeDtypeStruct((tokens, model), wide),
            jax.ShapeDtypeStruct((8, units), wide),
        ],
        compiler_params=pltpu.CompilerParams(vmem_limit_bytes=58 * 2**20),
        cost_estimate=pl.CostEstimate(
            flops=8 * tokens * model * units,
            bytes_accessed=20 * 2**20,
            transcendentals=2 * tokens * units,
        ),
    )(feed_in, upstream, expand, thresholds.reshape(1, units), contract)


def attention_kernel(n, per_device, slots, *refs):
    received, refs = refs[:n], refs[n:]
    cosine, sine = refs[0], refs[1]
    outs, refs = refs[2 : 2 + n], refs[2 + n :]
    xs, ys, k_lo, q_lo, v_hi, g_hi, k_turned, v_turned, strip, sums, sems = refs
    blocks = n * per_device
    span = xs.shape[3]
    tiles, big = strip.shape[0], strip.shape[1]
    ratio = big // span
    scale = HEAD_DIM ** (-0.5)
    to_log2 = scale * float(np.log2(np.e))

    copies = [pltpu.make_async_copy(received[k], xs.at[k], sems.at[k]) for k in range(n)]
    for copy in copies:
        copy.start()
    sums[...] = jnp.zeros_like(sums)
    for copy in copies:
        copy.wait()

    def place(j):
        slot = slots[j]
        return slot // per_device, slot % per_device

    def rows_of(u, size):
        return pl.ds(pl.multiple_of(u * size, size), size)

    lower = half_lanes((span, LANES))

    def order(j, _):
        a, b = place(j)
        rows = rows_of(j, span)
        x, y = xs[a, 0, b].astype(wide), xs[a, 1, b].astype(wide)
        k_lo[rows] = swap_halves(x).astype(low)
        q_lo[rows] = jnp.where(lower, x, 0.0).astype(low)
        v_hi[rows] = swap_halves(y).astype(low)
        g_hi[rows] = jnp.where(lower, 0.0, y).astype(low)
        return 0

    lax.fori_loop(0, blocks, order, 0)

    def turn(u, _):
        rows = rows_of(u, big)
        k_turned[u] = k_lo[rows].astype(wide).T[:HEAD_DIM].astype(low)
        v_turned[u] = v_hi[rows].astype(wide).T[HEAD_DIM:].astype(low)
        return 0

    lax.fori_loop(0, tiles, turn, 0)
    allowed = lax.broadcasted_iota(jnp.int32, (big, big), 0) <= lax.broadcasted_iota(
        jnp.int32, (big, big), 1
    )
    lower_big = half_lanes((big, LANES))

    def query_tile(u, _):
        own = rows_of(u, big)
        q, g = q_lo[own], g_hi[own]
        g_turned = g.astype(wide).T[HEAD_DIM:]

        s = jnp.where(allowed, dot_nt(k_lo[own], q), masked_value)
        strip[u] = s
        top = jnp.max(s, axis=0, keepdims=True)

        def scores(j, top):
            s = dot_nt(k_lo[rows_of(j, big)], q)
            strip[j] = s
            return jnp.maximum(top, jnp.max(s, axis=0, keepdims=True))

        top = lax.fori_loop(0, u, scores, top)

        def weigh(j, carry):
            total, out = carry
            p = jnp.exp2((strip[j] - top) * to_log2)
            strip[j] = p
            return total + jnp.sum(p, axis=0, keepdims=True), out + dot_nn(
                v_turned[j], p.astype(low)
            )

        zeros = jnp.zeros((HEAD_DIM, big), wide)
        total, out = lax.fori_loop(0, u + 1, weigh, (jnp.zeros((1, big), wide), zeros))
        recip = 1.0 / total
        out = out * recip
        slope_scale = scale * recip
        slope_shift = slope_scale * jnp.sum(out * g_turned, axis=0, keepdims=True)

        def back(j, dq):
            p = strip[j]
            dots = dot_nt(v_hi[rows_of(j, big)], g)
            slopes = (p * (dots * slope_scale - slope_shift)).astype(low)
            sums[j] += dot_nn(slopes, q) + dot_nn((p * recip).astype(low), g)
            return dq + dot_nn(k_turned[j], slopes)

        dq = lax.fori_loop(0, u + 1, back, zeros)
        packed = jnp.concatenate([out, dq], axis=0).T
        packed = jnp.where(lower_big, packed, rotate_lanes(packed, cosine[own], -sine[own]))
        packed = packed.astype(low)
        for t in range(ratio):
            a, b = place(u * ratio + t)
            ys[a, 0, b] = packed[t * span : (t + 1) * span]
        return 0

    lax.fori_loop(0, tiles, query_tile, 0)

    def finish(u, _):
        own = rows_of(u, big)
        x = sums[u]
        packed = jnp.where(lower_big, rotate_lanes(x, cosine[own], -sine[own]), x).astype(low)
        for t in range(ratio):
            a, b = place(u * ratio + t)
            ys[a, 1, b] = packed[t * span : (t + 1) * span]
        return 0

    lax.fori_loop(0, tiles, finish, 0)
    copies = [pltpu.make_async_copy(ys.at[k], outs[k], sems.at[k]) for k in range(n)]
    for copy in copies:
        copy.start()
    for copy in copies:
        copy.wait()


def attention(received, slots, tables, per_device):
    n = len(received)
    span = received[0].shape[2]
    blocks = n * per_device
    length = blocks * span
    big = span * (2 if blocks % 2 == 0 else 1)
    tiles = length // big
    anywhere = pl.BlockSpec(memory_space=pl.ANY)
    vmem = pl.BlockSpec(memory_space=pltpu.VMEM)
    pairs = tiles * (tiles + 1) // 2 * big * big
    turned = pltpu.VMEM((length, LANES), low)
    return pl.pallas_call(
        functools.partial(attention_kernel, n, per_device),
        in_specs=[pl.BlockSpec(memory_space=pltpu.SMEM)] + [anywhere] * n + [vmem] * 2,
        out_specs=[anywhere] * n,
        out_shape=[jax.ShapeDtypeStruct(received[0].shape, low)] * n,
        scratch_shapes=[
            pltpu.VMEM((n,) + received[0].shape, low),
            pltpu.VMEM((n,) + received[0].shape, low),
            turned,
            turned,
            turned,
            turned,
            pltpu.VMEM((tiles, HEAD_DIM, big), low),
            pltpu.VMEM((tiles, HEAD_DIM, big), low),
            pltpu.VMEM((tiles, big, big), wide),
            pltpu.VMEM((tiles, big, LANES), wide),
            pltpu.SemaphoreType.DMA((n,)),
        ],
        compiler_params=pltpu.CompilerParams(vmem_limit_bytes=40 * 2**20),
        cost_estimate=pl.CostEstimate(
            flops=12 * pairs * 512, bytes_accessed=8 * 2**20, transcendentals=pairs
        ),
    )(slots, *received, *tables)


def close_kernel(
    back, mix, proj, out, part, res, scale, both, attended_out, linear_out, sums, offs
):
    heads = back.shape[0]
    model = res.shape[2]
    normed = normalize_block(res[0].astype(wide))
    kinds = []
    for kind in range(2):
        kinds += unpack_heads([back[h, kind, 0].astype(wide) for h in range(heads)])
    attended, linear = kinds[0].astype(low), [x.astype(low) for x in kinds[1:]]
    attended_out[...] = attended
    both[:, :model] = (dot_nn(attended, mix[...]) + out[...]).astype(low)
    attn_part = sum(dot_nt(linear[i], proj[i]) for i in range(3))
    feed_part = part[...]
    both[:, model:] = (attn_part * scale[0:1] + feed_part * scale[1:2]).astype(low)

    @pl.when(pl.program_id(0) == 0)
    def _():
        sums[...] = jnp.zeros_like(sums)
        offs[...] = jnp.zeros_like(offs)

    for i in range(3):
        linear_out[i] = linear[i]
        offs[i : i + 1] += jnp.sum(kinds[1 + i].astype(low).astype(wide), axis=0, keepdims=True)
    for i, x in enumerate([attn_part * normed, feed_part * normed, attn_part, feed_part]):
        sums[i : i + 1] += jnp.sum(x, axis=0, keepdims=True)


def close(back, mixing, projections, out, part, residual, scale, first):
    heads, _, per_device, span, _ = back.shape
    local, model = mixing.shape
    whole = lambda *shape: pl.BlockSpec(shape, lambda t: (0,) * len(shape))
    rows = lambda columns: pl.BlockSpec((span, columns), lambda t: (t, 0))
    later = lambda columns: pl.BlockSpec((span, columns), lambda t: (first + t, 0))
    count = per_device * span
    return pl.pallas_call(
        close_kernel,
        grid=(per_device,),
        in_specs=[
            pl.BlockSpec((heads, 2, 1, span, LANES), lambda t: (0, 0, t, 0, 0)),
            whole(local, model),
            whole(3, model, local),
            later(model),
            later(model),
            pl.BlockSpec((1, span, model), lambda t: (first + t, 0, 0)),
            whole(2, model),
        ],
        out_specs=[
            rows(2 * model),
            rows(local),
            pl.BlockSpec((3, span, local), lambda t: (0, t, 0)),
            whole(8, model),
            whole(8, local),
        ],
        out_shape=[
            jax.ShapeDtypeStruct((count, 2 * model), low),
            jax.ShapeDtypeStruct((count, local), low),
            jax.ShapeDtypeStruct((3, count, local), low),
            jax.ShapeDtypeStruct((8, model), wide),
            jax.ShapeDtypeStruct((8, local), wide),
        ],
        compiler_params=pltpu.CompilerParams(vmem_limit_bytes=58 * 2**20),
        cost_estimate=pl.CostEstimate(
            flops=8 * count * model * local, bytes_accessed=12 * 2**20, transcendentals=0
        ),
    )(back, mixing, projections, out, part, residual, scale)


def steps_over(*axes):
    steps = []
    for axis in axes:
        size = lax.axis_size(axis)
        bit = 1
        while bit < size:
            steps.append((axis, [(s, s ^ bit) for s in range(size)], bit))
            bit *= 2
    return steps


def side_of(axis, bit):
    return (lax.axis_index(axis) // bit) % 2


def after(x, earlier):
    first = earlier[(0,) * earlier.ndim].astype(wide)
    return x + jnp.minimum(jnp.abs(first), 0.0).astype(x.dtype)


class RowSum:
    def __init__(self, x, steps, middle=lambda x: x):
        self.x, self.steps, self.middle = x, steps, middle
        self.sent = None
        self.at = 0

    def step(self, earlier=None):
        count = len(self.steps)
        if self.done():
            return
        if self.at < count:
            axis, perm, bit = self.steps[self.at]
            half = self.x.shape[0] // 2
            side = side_of(axis, bit)
            sent = lax.dynamic_slice_in_dim(self.x, (1 - side) * half, half, 0).astype(low)
            kept = lax.dynamic_slice_in_dim(self.x, side * half, half, 0)
            if earlier is not None:
                sent = after(sent, earlier)
            self.sent = sent
            got = lax.ppermute(sent, axis, perm)
            self.x = kept.astype(wide) + got.astype(wide)
            if self.at == count - 1:
                self.x = self.middle(self.x).astype(low)
        else:
            axis, perm, bit = self.steps[2 * count - 1 - self.at]
            x = self.x if earlier is None else after(self.x, earlier)
            self.sent = x
            got = lax.ppermute(x, axis, perm)
            self.last = (side_of(axis, bit), x, got)
            self.x = jnp.where(
                side_of(axis, bit) == 0,
                jnp.concatenate([x, got], axis=0),
                jnp.concatenate([got, x], axis=0),
            )
        self.at += 1

    def done(self):
        return self.at >= 2 * len(self.steps)


def own_rows(x, steps):
    for axis, _, bit in steps:
        half = x.shape[0] // 2
        x = lax.dynamic_slice_in_dim(x, side_of(axis, bit) * half, half, 0)
    return x


def sum_small(x, steps):
    for axis, perm, _ in steps:
        x = x + lax.ppermute(x, axis, perm)
    return x


def on_device(
    residual,
    block_order,
    projections,
    offsets,
    mixing,
    baseline,
    expand,
    thresholds,
    contract,
    norm_scale,
    norm_shift,
    cotangent,
):
    seq_count, local_rows, model = residual.shape
    local = mixing.shape[0]
    heads = local // HEAD_DIM
    n = lax.axis_size("seq")
    me = lax.axis_index("seq")
    blocks = block_order.shape[1]
    length = local_rows * n
    span = length // blocks
    per_device = blocks // n
    tokens = seq_count * local_rows
    rounds = seq_count * heads // n
    tables = [jnp.asarray(t) for t in rotary_tables(length)]
    batch_steps = steps_over("dp", "seq")
    tensor_steps = steps_over("tensor")

    own_blocks = lax.dynamic_slice_in_dim(block_order, me * per_device, per_device, 1).reshape(-1)
    residual_blocks = residual.reshape(seq_count * per_device, span, model)
    sends, attn_in, feed_in = project(
        residual_blocks,
        cotangent.reshape(residual_blocks.shape),
        own_blocks,
        projections,
        offsets,
        mixing,
        norm_scale,
        norm_shift,
        tables,
        (seq_count, per_device, heads),
    )
    received = []
    for r in range(rounds):
        first = r * n
        received.append([lax.dynamic_index_in_dim(sends, r * n + me, 0, keepdims=False)])
        for k in range(1, n):
            part = lax.dynamic_index_in_dim(sends, first + (me + k) % n, 0, keepdims=False)
            received[r].append(lax.ppermute(part, "seq", [(s, (s + k) % n) for s in range(n)]))

    stored = jnp.arange(blocks, dtype=jnp.int32)
    slot_of = ((me - stored // per_device) % n) * per_device + stored % per_device

    def slots_in(r):
        order = lax.dynamic_index_in_dim(block_order, (r * n + me) // heads, 0, keepdims=False)
        return jnp.sum(
            jnp.where(order[None, :] == stored[:, None], slot_of[None, :], 0), axis=1
        ).astype(jnp.int32)

    attn_in = attn_in.reshape(tokens, model)
    feed_in = feed_in.reshape(tokens, model)
    upstream_low = cotangent.reshape(tokens, model)
    activated, grad_hidden, feed_out, feed_part, feed_sums = feed_forward(
        feed_in, upstream_low, expand, thresholds, contract, span
    )

    def dot_tn(a, b):
        return lax.dot_general(a, b, (((0,), (0,)), ((), ())), preferred_element_type=wide)

    grad_contract = lax.psum(dot_tn(activated, upstream_low).astype(low), ("dp", "seq"))
    expand_sum = RowSum(
        dot_tn(feed_in, grad_hidden),
        steps_over("dp"),
        lambda x: lax.psum(x.astype(low), "seq"),
    )
    for _ in expand_sum.steps:
        expand_sum.step()

    back = []
    for r in range(rounds):
        pieces = attention(received[r], slots_in(r), tables, per_device)
        full = jnp.zeros((n,) + pieces[0].shape, low)
        for k in range(n):
            piece = pieces[k]
            if k:
                piece = lax.ppermute(piece, "seq", [(s, (s - k) % n) for s in range(n)])
            full = lax.dynamic_update_index_in_dim(full, piece, (me + k) % n, 0)
        back.append(full)

    flat_residual = residual.reshape(tokens, model)

    def finish(mine, totals):
        inputs = own_rows(flat_residual[mine], tensor_steps).astype(wide)
        layer_own = inputs + totals[:, :model] + baseline
        combined = totals[:, model:]
        centred = inputs - jnp.mean(inputs, axis=-1, keepdims=True)
        inverse = lax.rsqrt(jnp.mean(centred * centred, axis=-1, keepdims=True) + norm_eps)
        normed = centred * inverse
        grad_own = own_rows(upstream_low[mine], tensor_steps).astype(wide) + inverse * (
            combined
            - jnp.mean(combined, axis=-1, keepdims=True)
            - normed * jnp.mean(combined * normed, axis=-1, keepdims=True)
        )
        return jnp.concatenate([layer_own.astype(low), grad_own.astype(low)], axis=1)

    small_sums, branches, attended, grad_linear = [], [], [], []
    for s in range(seq_count):
        pairs = range(s * heads, (s + 1) * heads)
        if heads % n == 0:
            pieces = [back[r] for r in range(s * heads // n, (s + 1) * heads // n)]
            pairs_back = pieces[0] if len(pieces) == 1 else jnp.concatenate(pieces, axis=0)
        else:
            pairs_back = jnp.stack([back[p // n][p % n] for p in pairs])
        both, attended_s, linear_s, sums_s, offs_s = close(
            pairs_back,
            mixing,
            projections,
            feed_out,
            feed_part,
            residual_blocks,
            after(norm_scale, branches[-1].sent) if branches else norm_scale,
            s * per_device,
        )
        attended.append(attended_s)
        grad_linear.append(linear_s)
        small_sums.append((sums_s, offs_s))
        mine = slice(s * local_rows, (s + 1) * local_rows)
        branches.append(RowSum(both, tensor_steps, functools.partial(finish, mine)))
        branches[s].step()
        if s < seq_count - 1:
            branches[s].step()

    attended = jnp.concatenate(attended, axis=0)
    grad_linear = jnp.concatenate(grad_linear, axis=1)
    sums = sum_small(sum(s for s, _ in small_sums)[:4], tensor_steps)
    grad_offsets = sum(o for _, o in small_sums)[:3]
    small = jnp.concatenate(
        [sums.reshape(-1), grad_offsets.reshape(-1), feed_sums[0], feed_sums[1]]
    )
    shares = 1
    for _ in batch_steps:
        shares *= 2
    unit = model * shares
    padded = -(-small.shape[0] // unit) * unit
    small_rows = jnp.pad(small, (0, padded - small.shape[0])).reshape(-1, model)
    params = [
        RowSum(
            jnp.concatenate([dot_tn(attn_in, grad_linear[i]) for i in range(3)], axis=0),
            batch_steps,
        ),
        RowSum(
            jnp.concatenate([dot_tn(attended, upstream_low), small_rows], axis=0), batch_steps
        ),
    ]
    params[0].step()
    params[1].step(params[0].sent)
    grad_contract = grad_contract.astype(wide)
    turn = 0
    while not all(b.done() for b in branches + params + [expand_sum]):
        for chain in branches[::-1]:
            chain.step()
        last = params[0].at == 2 * len(batch_steps) - 1
        params[0].step(grad_contract if last else None)
        if not params[1].done():
            params[1].step(params[0].sent)
        turn += 1
        if turn > 1:
            expand_sum.step(params[0].sent)
    grad_expand = expand_sum.x.astype(wide)

    layer_output = jnp.zeros((seq_count, local_rows, model), low)
    grad_residual = layer_output
    for s, chain in enumerate(branches):
        side, *pieces = chain.last
        for position, piece in zip((side, 1 - side), pieces):
            at = (s, position * piece.shape[0], 0)
            layer_output = lax.dynamic_update_slice(layer_output, piece[None, :, :model], at)
            grad_residual = lax.dynamic_update_slice(grad_residual, piece[None, :, model:], at)
    grad_projections = params[0].x.astype(wide).reshape(3, model, local)
    small = params[1].x[local:].astype(wide).reshape(-1)
    grad_mixing = params[1].x[:local].astype(wide)
    sizes = [2 * model, 2 * model, 3 * local, thresholds.shape[0], model]
    cuts = np.cumsum(sizes)
    grad_scale, grad_shift, grad_offsets, grad_thresholds, grad_baseline = jnp.split(
        small[: cuts[-1]], cuts[:-1]
    )
    return (
        layer_output,
        grad_residual,
        grad_projections,
        grad_offsets.reshape(3, local),
        grad_mixing,
        grad_baseline,
        grad_expand,
        grad_thresholds,
        grad_contract,
        grad_scale.reshape(2, model),
        grad_shift.reshape(2, model),
    )


def solution(mesh):
    in_specs = (
        P("dp", "seq", None),
        P("dp", None),
        P(None, None, "tensor"),
        P(None, "tensor"),
        P("tensor", None),
        P(),
        P(None, "tensor"),
        P("tensor"),
        P("tensor", None),
        P(),
        P(),
        P("dp", "seq", None),
    )
    out_specs = (
        P("dp", "seq", None),
        P("dp", "seq", None),
        P(None, None, "tensor"),
        P(None, "tensor"),
        P("tensor", None),
        P(),
        P(None, "tensor"),
        P("tensor"),
        P("tensor", None),
        P(),
        P(),
    )
    return jax.shard_map(
        on_device, mesh=mesh, in_specs=in_specs, out_specs=out_specs, check_vma=False
    )
```
